32 devices in a mesh: rows: 8 (over z, y), rhs: 4 (over x, core).
Axes of the slice: x: 2, y: 2, z: 4, core: 2. Of those that a mesh axis runs over, the one named last changes fastest.
Arguments:
- factor_left: bfloat16 [1024, 128, 128], P(('rows', 'rhs')), may hold values from -0.5 to 0.5
- factor_right: bfloat16 [1024, 128, 128], P(('rows', 'rhs')), may hold values from -0.5 to 0.5
- state_diag: float32 [1024, 128], P(('rows', 'rhs')), may hold values from 0.02 to 0.2
- owner: int32 [1024, 1], P(('rows', 'rhs')), may hold values from 0 to 7; in each aligned block of 32 rows (0 to 31, 32 to 63, ...) at most 12 rows name the same one
- col_local: int32 [1024], P(('rows', 'rhs')), may hold values from 0 to 15
- row_shift: int32 [1024], P(('rows', 'rhs')), may hold values from 0 to 2
- row_local: int32 [1024], P(('rows', 'rhs')), may hold values from 0 to 15
- rhs_in: float32 [128, 256, 128], P('rows', 'rhs'), may hold values from -6 to 6
- low_bound: float32 [1], replicated, may hold values from 0.55 to 0.7
- high_bound: float32 [1], replicated, may hold values from 1.3 to 1.5
Outputs:
- adjoint: float32 [128, 256, 128], P('rows', 'rhs')
- residual: float32 [128, 256, 128], P('rows', 'rhs')
The draws below stay inside these ranges and needn't reach their ends.
Inputs may be any that keep to these rules, and one draw needn't show every extreme that they name: Among the 32 blocks of one device no owner is named more than 12 times, and every draw has a device that names some owner 12 times.
All inputs are finite; a program needn't handle non-finite values.
Results may differ from the reference program's by a relative error of at most 0.0082.
Values may be sent and summed in bfloat16 or wider, within the bound.
A program may use at most 128 MiB of HBM per device.

```python
import math
import jax
import jax.numpy as jnp
import numpy as np
from jax import lax

BS = 128
RHS = 256
ITERS = 4
ROWS_DEV = 16
SLOT_DEV = 32
CAP = 12
NB = 128
NNZ = 1024
N_ROWS = 8


def set_ends(result, stream_key, smallest, largest):
    extent = result.shape
    spot = [jax.random.randint(jax.random.fold_in(stream_key, axis), (), 0, extent[axis]) for axis in range(len(extent))]
    result = result.at[tuple(spot)].set(smallest)
    longest = extent.index(max(extent))
    spot[longest] = (spot[longest] + 1) % extent[longest]
    return result.at[tuple(spot)].set(largest)


def shard_levels(rng, extent, shards, least, top_value):
    gain = 1.0
    for dim, blocks in shards:
        heights = jax.random.uniform(jax.random.fold_in(jax.random.fold_in(rng, 6), dim), (blocks,), jnp.float32, least / len(shards), top_value / len(shards))
        gain = gain * jnp.repeat(jnp.exp(heights), extent[dim] // blocks).reshape((-1,) + (1,) * (len(extent) - 1 - dim))
    return gain


def routed_block(own_key, own, number, rows, amount, top, most, slope):
    sequence = jax.random.permutation(own_key, amount)
    heavy_load, common = load_shares(amount, rows * top, most, slope, True), load_shares(amount, rows * top, most, slope, False)
    places = jnp.arange(amount)

    def named(lengths, offset_by):
        used = int((lengths > 0).sum())
        fixed = max(1, used // 4)
        shifted = fixed + (places - fixed + offset_by * (used - fixed)) % max(1, amount - fixed)
        return jnp.zeros((amount,), jnp.int32).at[sequence[jnp.where(places < fixed, places, shifted)]].set(jnp.asarray(lengths, jnp.int32))

    lengths = jnp.where(number % 4 == 0, named(heavy_load, number // 4), named(common, number - number // 4 - 1))
    mixed = jax.random.permutation(jax.random.fold_in(own, 3), amount)
    giver, taker = mixed[0:amount // 2 * 2:2], mixed[1:amount // 2 * 2:2]
    room = jnp.minimum(lengths[giver] - 1, most - lengths[taker]) // 2
    room = jnp.where((giver == sequence[0]) | (taker == sequence[0]) | (lengths[taker] == 0), 0, jnp.maximum(room, 0))
    shifted = jax.random.randint(jax.random.fold_in(own, 4), (amount // 2,), 0, 1 << 20) % (room + 1)
    lengths = lengths.at[giver].add(-shifted).at[taker].add(shifted)
    labels = jnp.searchsorted(jnp.cumsum(lengths), jnp.arange(rows * top), side="right").astype(jnp.int32)
    table = labels.reshape(top, rows).T
    table = table[jax.random.permutation(jax.random.fold_in(own, 1), rows)]
    offset_by = jax.random.randint(jax.random.fold_in(own, 2), (rows, 1), 0, top)
    return jnp.take_along_axis(table, (jnp.arange(top)[None, :] + offset_by) % top, axis=1)


def load_shares(number_of, total, most, skew, full):
    weights = [(1 << 20) // math.isqrt(rank ** skew) + 1 for rank in range(1, number_of + 1)]
    largest = most if full else min(most, max(-(-total // number_of), total * weights[0] // sum(weights)))
    least = 1 if total - largest >= number_of - 1 else 0
    holding, rest = [largest] + [least] * (number_of - 1), total - largest - least * (number_of - 1)
    while rest > 0:
        free = [i for i in range(1, number_of) if holding[i] < largest] or [i for i in range(1, number_of) if holding[i] < most]
        whole, budget = sum([weights[i] for i in free]), rest
        for i in free:
            extra = min(most - holding[i], max(1, budget * weights[i] // whole), rest)
            holding[i] = holding[i] + extra
            rest = rest - extra
    return np.array(holding)


def scatter_about(rng, extent, scale, most, shards=(), held_as=jnp.bfloat16):
    factor_of = shard_levels(rng, extent, shards, -0.22, 0.18) if shards else 1.0
    array = jax.random.normal(rng, extent, jnp.float32) * scale * factor_of
    return jnp.minimum(jnp.maximum(array, -most), most).astype(held_as)


def setup_inputs(seed: int = 0) -> dict:
    splits = jax.random.split(jax.random.key(seed), 11)
    factor_left = scatter_about(splits[0], (NNZ, BS, BS), BS ** -0.5, 0.5, ((0, 32),))
    factor_right = scatter_about(splits[1], (NNZ, BS, BS), BS ** -0.5, 0.5, ((0, 32),))
    state_diag = jnp.clip(jnp.exp(math.log(0.2) - 2.3025851 * jax.random.uniform(splits[2], (NNZ, BS), jnp.float32) ** shard_levels(splits[2], (NNZ, BS), ((0, 32),), -0.2, 0.2)), 0.02, 0.2)
    owner_keys = jax.random.split(jax.random.fold_in(splits[3], 1), NNZ // SLOT_DEV)
    owner_turns = jax.random.permutation(jax.random.fold_in(splits[3], 3), NNZ // SLOT_DEV)
    owner = jax.vmap(lambda own, number: routed_block(jax.random.fold_in(splits[3], 2), own, number, SLOT_DEV, N_ROWS, 1, CAP, 2))(owner_keys, owner_turns).reshape((NNZ, 1))
    col_local = set_ends(jax.random.randint(splits[4], (NNZ,), 0, ROWS_DEV), jax.random.fold_in(splits[4], 1), 0, ROWS_DEV - 1).astype(jnp.int32)
    row_shift = set_ends(jax.random.randint(splits[5], (NNZ,), 0, 3), jax.random.fold_in(splits[5], 1), 0, 2).astype(jnp.int32)
    row_local = set_ends(jax.random.randint(splits[6], (NNZ,), 0, ROWS_DEV), jax.random.fold_in(splits[6], 1), 0, ROWS_DEV - 1).astype(jnp.int32)
    rhs_in = scatter_about(splits[7], (NB, RHS, BS), 1.0, 6.0, ((0, 8), (1, 4)), jnp.float32)
    low_bound = jnp.clip(jax.random.uniform(splits[8], (1,), jnp.float32, 0.55, 0.7), 0.55, 0.7)
    high_bound = jnp.clip(jax.random.uniform(splits[9], (1,), jnp.float32, 1.3, 1.5), 1.3, 1.5)
    return dict(factor_left=factor_left, factor_right=factor_right, state_diag=state_diag, owner=owner, col_local=col_local, row_shift=row_shift, row_local=row_local, rhs_in=rhs_in, low_bound=low_bound, high_bound=high_bound)


def form_group(items):
    left, right, diag = items
    scaled = (diag[:, :, None] * right.astype(jnp.float32)).astype(jnp.bfloat16)
    scaled = lax.optimization_barrier(scaled)
    product = jnp.einsum('kam,kmb->kab', left.astype(jnp.float32), scaled.astype(jnp.float32), precision=lax.Precision.HIGHEST)
    return product.astype(jnp.bfloat16)


def reference(factor_left, factor_right, state_diag, owner, col_local, row_shift, row_local, rhs_in, low_bound, high_bound):
    group = math.gcd(NNZ, 256)
    count = NNZ // group
    blocks = lax.map(form_group, (factor_left.reshape(count, group, BS, BS), factor_right.reshape(count, group, BS, BS), state_diag.reshape(count, group, BS)))
    dest = owner[:, 0].astype(jnp.int32)
    col_index = (dest * ROWS_DEV + col_local).astype(jnp.int32)
    row_index = ((dest + row_shift - 1) * ROWS_DEV + row_local) % NB
    row_index = row_index.astype(jnp.int32)
    col_groups = col_index.reshape(count, group)
    row_groups = row_index.reshape(count, group)

    def apply_operator(field):
        rounded = lax.optimization_barrier(field.astype(jnp.bfloat16)).astype(jnp.float32)

        def add_group(total, items):
            blk, rows_here, cols_here = items
            picked = rounded[rows_here]
            product = jnp.einsum('khb,kbc->khc', picked, blk.astype(jnp.float32), precision=lax.Precision.HIGHEST)
            return total.at[cols_here].add(product), None

        total, _ = lax.scan(add_group, jnp.zeros_like(field), (blocks, row_groups, col_groups))
        return field - total

    low = low_bound[0]
    high = high_bound[0]
    theta = (high + low) / 2.0
    delta = (high - low) / 2.0
    sigma = theta / delta
    rho = 1.0 / sigma
    adjoint = jnp.zeros_like(rhs_in)
    residual = rhs_in
    direction = residual / theta
    for sweep in range(ITERS):
        adjoint = adjoint + direction
        residual = residual - apply_operator(direction)
        if sweep + 1 < ITERS:
            rho_next = 1.0 / (2.0 * sigma - rho)
            direction = rho_next * rho * direction + (2.0 * rho_next / delta) * residual
            rho = rho_next
    return adjoint, residual
```

```python
import functools

import jax
import jax.numpy as jnp
from jax import lax
from jax.experimental import pallas as pl
from jax.experimental.pallas import tpu as pltpu
from jax.sharding import PartitionSpec as P

ITERS = 4
GROUP = 16


def make_buckets(blocks, dest, place, peers, room):
    slots = dest.shape[0]
    width = blocks.shape[1]
    target = dest * room + place
    select = jnp.arange(peers * room)[:, None] == target[None, :]
    moved = jnp.dot(
        select.astype(jnp.bfloat16),
        blocks.reshape(slots, width * width),
        preferred_element_type=jnp.float32,
    ).astype(jnp.bfloat16)
    return moved.reshape(peers, room, width, width)


def bits_of(local_rows):
    return (2 * local_rows - 1).bit_length(), local_rows.bit_length()


def block_list(mine, slot, col, index, local_rows, total):
    index_bits, col_bits = bits_of(local_rows)
    counts = jnp.sum(mine.astype(jnp.int32), axis=1)
    devices, slots = mine.shape
    before = jnp.arange(devices)[:, None] > jnp.arange(devices)[None, :]
    first = jnp.sum(jnp.where(before, counts[None, :], 0), axis=1)
    earlier = jnp.arange(slots)[:, None] > jnp.arange(slots)[None, :]
    inside = jnp.sum((earlier[None] & mine[:, None, :]).astype(jnp.int32), axis=2)
    pos = jnp.where(mine, first[:, None] + inside, -1).reshape(-1)
    value = ((slot << col_bits) | col) << index_bits | index
    empty = local_rows << index_bits
    pick = jnp.arange(total)[:, None] == pos[None, :]
    listed = empty + jnp.sum(jnp.where(pick, value.reshape(1, -1) - empty, 0), axis=1)
    return listed, jnp.sum(counts).reshape(1)


def add_blocks(list_ref, count_ref, blocks_ref, read, acc, buf, sems, local_rows):
    index_bits, col_bits = bits_of(local_rows)
    chunks = lax.div(count_ref[0] + (GROUP - 1), jnp.int32(GROUP))

    def copy(chunk, slot, g):
        where = list_ref[chunk * GROUP + g] >> (index_bits + col_bits)
        return pltpu.make_async_copy(blocks_ref.at[where], buf.at[slot, g], sems.at[slot, g])

    def start(chunk, slot):
        for g in range(GROUP):
            copy(chunk, slot, g).start()

    @pl.when(chunks > 0)
    def _():
        start(0, 0)

    def body(chunk, carry):
        slot = lax.rem(chunk, 2)

        @pl.when(chunk + 1 < chunks)
        def _():
            start(chunk + 1, 1 - slot)

        for g in range(GROUP):
            copy(chunk, slot, g).wait()
        for g in range(GROUP):
            item = list_ref[chunk * GROUP + g]
            row = item & ((1 << index_bits) - 1)
            col = (item >> index_bits) & ((1 << col_bits) - 1)
            acc[col] += jnp.dot(read[row], buf[slot, g], preferred_element_type=jnp.float32)
        return carry

    lax.fori_loop(0, chunks, body, 0)


def near_kernel(list_ref, count_ref, blocks_ref, own_ref, dir_ref, res_ref, out_ref, acc, buf, sems):
    rows = dir_ref.shape[0]
    acc[0:rows] = res_ref[...] - dir_ref[...]
    add_blocks(list_ref, count_ref, blocks_ref, own_ref, acc, buf, sems, rows)
    out_ref[...] = acc[0:rows]


def far_kernel(last, list_ref, count_ref, coef_ref, blocks_ref, low_ref, high_ref, part_ref, *rest):
    if last:
        res_out, ext, acc, buf, sems, ext_sems = rest
    else:
        dir_ref, adj_ref, res_out, dir_out, adj_out, round_out, ext, acc, buf, sems, ext_sems = rest
    rows = part_ref.shape[0]
    low = pltpu.make_async_copy(low_ref, ext.at[0:rows], ext_sems.at[0])
    high = pltpu.make_async_copy(high_ref, ext.at[rows : 2 * rows], ext_sems.at[1])
    low.start()
    high.start()
    acc[0:rows] = part_ref[...]
    low.wait()
    high.wait()
    add_blocks(list_ref, count_ref, blocks_ref, ext, acc, buf, sems, rows)
    res = acc[0:rows]
    res_out[...] = res
    if not last:
        direction = coef_ref[0] * dir_ref[...] + coef_ref[1] * res
        dir_out[...] = direction
        adj_out[...] = adj_ref[...] + direction
        round_out[...] = direction.astype(jnp.bfloat16)


def local(
    factor_left,
    factor_right,
    state_diag,
    owner,
    col_local,
    row_shift,
    row_local,
    rhs_in,
    low_bound,
    high_bound,
):
    peers = lax.axis_size("rows")
    sides = lax.axis_size("rhs")
    me = lax.axis_index("rows")
    slots = owner.shape[0]
    width = factor_left.shape[1]
    local_rows, columns, _ = rhs_in.shape
    room = min(slots, max(2, 3 * slots // peers))
    dest = owner[:, 0]

    packed = ((dest * local_rows + col_local) * 3 + row_shift) * local_rows + row_local
    table = lax.all_gather(packed, ("rows", "rhs"), axis=0, tiled=True).reshape(-1, slots)

    scaled = (state_diag[:, :, None] * factor_right).astype(jnp.bfloat16)
    blocks = jnp.einsum(
        "kam,kmb->kab", factor_left, scaled, preferred_element_type=jnp.float32
    ).astype(jnp.bfloat16)
    order = jnp.arange(slots)
    earlier = (dest[:, None] == dest[None, :]) & (order[None, :] < order[:, None])
    place = jnp.sum(earlier.astype(jnp.int32), axis=1)
    send_blocks = make_buckets(blocks, dest, place, peers, room)
    mine_blocks = lax.all_to_all(send_blocks, "rows", split_axis=0, concat_axis=0, tiled=True)
    got_blocks = lax.all_gather(mine_blocks, "rhs", axis=1, tiled=True)
    got_blocks = got_blocks.reshape(peers * sides * room, width, width)

    row_all = table % local_rows
    shift_all = (table // local_rows) % 3
    col_all = (table // (3 * local_rows)) % local_rows
    own_all = table // (3 * local_rows * local_rows)
    same = (own_all[:, :, None] == own_all[:, None, :]) & (order[None, :] < order[:, None])[None]
    place_all = jnp.sum(same.astype(jnp.int32), axis=2)
    slot_all = jnp.arange(table.shape[0])[:, None] * room + place_all
    index_all = row_all + jnp.where(shift_all == 2, local_rows, 0)
    total = -(-peers * sides * room // GROUP) * GROUP
    mine = own_all == me
    near_list, near_count = block_list(
        mine & (shift_all == 1), slot_all, col_all, index_all, local_rows, total
    )
    far_list, far_count = block_list(
        mine & (shift_all != 1), slot_all, col_all, index_all, local_rows, total
    )

    low = low_bound[0]
    high = high_bound[0]
    theta = (high + low) / 2.0
    delta = (high - low) / 2.0
    sigma = theta / delta
    rho = 1.0 / sigma
    residual = rhs_in
    direction = residual / theta
    adjoint = direction
    rounded = direction.astype(jnp.bfloat16)

    forward = [(i, (i + 1) % peers) for i in range(peers)]
    backward = [(i, (i - 1) % peers) for i in range(peers)]
    smem = pl.BlockSpec(memory_space=pltpu.SMEM)
    vmem = pl.BlockSpec(memory_space=pltpu.VMEM)
    hbm = pl.BlockSpec(memory_space=pl.ANY)
    field = jax.ShapeDtypeStruct(rhs_in.shape, jnp.float32)
    work = [
        pltpu.VMEM((local_rows + 1, columns, width), jnp.float32),
        pltpu.VMEM((2, GROUP, width, width), jnp.bfloat16),
        pltpu.SemaphoreType.DMA((2, GROUP)),
    ]
    params = pltpu.CompilerParams(vmem_limit_bytes=24 * 1024 * 1024)

    def cost(amount):
        return pl.CostEstimate(
            flops=2 * amount * columns * width * width,
            bytes_accessed=amount * width * width * 2 + 4 * rhs_in.size * 4,
            transcendentals=0,
        )

    for sweep in range(ITERS):
        last = sweep + 1 == ITERS
        low_rows = lax.ppermute(rounded, "rows", forward)
        high_rows = lax.ppermute(rounded, "rows", backward)
        part = pl.pallas_call(
            near_kernel,
            out_shape=field,
            in_specs=[smem, smem, hbm, vmem, vmem, vmem],
            out_specs=vmem,
            scratch_shapes=work,
            compiler_params=params,
            cost_estimate=cost(total // 6),
            name="near",
        )(near_list, near_count, got_blocks, rounded, direction, residual)
        if last:
            coef = jnp.zeros((2,), jnp.float32)
        else:
            rho_next = 1.0 / (2.0 * sigma - rho)
            coef = jnp.stack([rho_next * rho, 2.0 * rho_next / delta])
            rho = rho_next
        fields = [] if last else [direction, adjoint]
        outs = [field] if last else [field] * 3 + [jax.ShapeDtypeStruct(rhs_in.shape, jnp.bfloat16)]
        result = pl.pallas_call(
            functools.partial(far_kernel, last),
            out_shape=outs,
            in_specs=[smem, smem, smem, hbm, hbm, hbm, vmem] + [vmem] * len(fields),
            out_specs=[vmem] * len(outs),
            scratch_shapes=[pltpu.VMEM((2 * local_rows, columns, width), jnp.bfloat16)]
            + work
            + [pltpu.SemaphoreType.DMA((2,))],
            compiler_params=params,
            cost_estimate=cost(total // 3),
            name="far_last" if last else "far",
        )(far_list, far_count, coef, got_blocks, low_rows, high_rows, part, *fields)
        residual = result[0]
        if not last:
            _, direction, adjoint, rounded = result
    return (adjoint, residual)


def solution(mesh):
    placed = (
        P(("rows", "rhs"), None, None),
        P(("rows", "rhs"), None, None),
        P(("rows", "rhs"), None),
        P(("rows", "rhs"), None),
        P(("rows", "rhs")),
        P(("rows", "rhs")),
        P(("rows", "rhs")),
        P("rows", "rhs", None),
        P(),
        P(),
    )
    return jax.shard_map(
        local,
        mesh=mesh,
        in_specs=placed,
        out_specs=(P("rows", "rhs", None), P("rows", "rhs", None)),
        check_vma=False,
    )
```

```python
import functools

import jax
import jax.numpy as jnp
from jax import lax
from jax.experimental import pallas as pl
from jax.experimental.pallas import tpu as pltpu
from jax.sharding import PartitionSpec as P

ITERS = 4
GROUP = 16
BUFFERS = 4
MESH = pl.DeviceIdType.MESH


def bits_of(local_rows):
    return (2 * local_rows).bit_length(), local_rows.bit_length()


def make_buckets(blocks, dest, col, index, near, peers, room):
    slots = dest.shape[0]
    width = blocks.shape[1]
    order = jnp.arange(slots)
    earlier = (dest[:, None] == dest[None, :]) & (order[None, :] < order[:, None])
    place = jnp.sum(earlier.astype(jnp.int32), axis=1)
    target = dest * room + place
    select = jnp.arange(peers * room)[:, None] == target[None, :]
    moved = jnp.dot(
        select.astype(jnp.bfloat16),
        blocks.reshape(slots, width * width),
        preferred_element_type=jnp.float32,
    ).astype(jnp.bfloat16)
    picks = select.astype(jnp.int32)

    def spread(values):
        row = jnp.sum(picks * values[None, :], axis=1).reshape(peers, 1, room)
        return jnp.pad(row, ((0, 0), (0, 0), (0, width - room)))

    notes = jnp.concatenate(
        [spread(jnp.ones_like(dest)), spread(col), spread(index), spread(near)], axis=1
    )
    notes = jnp.pad(notes, ((0, 0), (0, 16 - 4), (0, 0))).astype(jnp.bfloat16)
    return jnp.concatenate([moved.reshape(peers, room * width, width), notes], axis=1)


def route_kernel(peers, sides, send_ref, got_ref, own_sem, send_sems, recv_sems):
    me, side = lax.axis_index("rows"), lax.axis_index("rhs")
    across, beside = side ^ 2, side ^ 1

    barrier = pltpu.get_barrier_semaphore()
    for d in range(1, peers):
        pl.semaphore_signal(
            barrier, inc=1, device_id=(lax.rem(me + d, peers), side), device_id_type=MESH
        )
    for other in (across, beside):
        pl.semaphore_signal(barrier, inc=1, device_id=(me, other), device_id_type=MESH)
    pl.semaphore_wait(barrier, peers + 1)

    def remote(kind, d, src, slot, device):
        return pltpu.make_async_remote_copy(
            src_ref=src,
            dst_ref=got_ref.at[slot],
            send_sem=send_sems.at[kind, d],
            recv_sem=recv_sems.at[kind, d],
            device_id=device,
            device_id_type=MESH,
        )

    def source(d):
        return lax.rem(me - d + peers, peers)

    def to_owner(d):
        owner = lax.rem(me + d, peers)
        return remote(0, d, send_ref.at[owner], me * sides + side, (owner, side))

    def held(d):
        return send_ref.at[me] if d == 0 else got_ref.at[source(d) * sides + side]

    def to_across(d):
        return remote(1, d, held(d), source(d) * sides + side, (me, across))

    def to_beside(d):
        return remote(2, d, held(d), source(d) * sides + side, (me, beside))

    def on_beside(d):
        slot = source(d) * sides + across
        return remote(3, d, got_ref.at[slot], slot, (me, beside))

    for d in range(1, peers):
        to_owner(d).start()
    own = pltpu.make_async_copy(send_ref.at[me], got_ref.at[me * sides + side], own_sem)
    own.start()
    for d in range(peers + 2):
        if d < peers:
            if d > 0:
                to_owner(d).wait_recv()
            to_across(d).start()
            to_beside(d).start()
        if d >= 2:
            to_across(d - 2).wait_recv()
            on_beside(d - 2).start()
    own.wait()
    for d in range(peers):
        if d > 0:
            to_owner(d).wait_send()
        to_across(d).wait_send()
        to_beside(d).wait()
        on_beside(d).wait()


def route(send, peers, sides):
    return pl.pallas_call(
        functools.partial(route_kernel, peers, sides),
        out_shape=jax.ShapeDtypeStruct((peers * sides,) + send.shape[1:], send.dtype),
        in_specs=[pl.BlockSpec(memory_space=pltpu.HBM)],
        out_specs=pl.BlockSpec(memory_space=pltpu.HBM),
        scratch_shapes=[
            pltpu.SemaphoreType.DMA,
            pltpu.SemaphoreType.DMA((4, peers)),
            pltpu.SemaphoreType.DMA((4, peers)),
        ],
        compiler_params=pltpu.CompilerParams(collective_id=0, has_side_effects=True),
        name="route",
    )(send)


def block_lists(notes, room, local_rows):
    index_bits, col_bits = bits_of(local_rows)
    filled, col, index, near = [notes[:, i, :room].reshape(-1) for i in range(4)]
    count = filled.shape[0]
    length = -(-(count + 2 * local_rows) // GROUP) * GROUP
    key = jnp.where(filled == 1, (1 - near) * local_rows + col, -1)
    items = jnp.arange(count)
    keys = jnp.arange(2 * local_rows)
    rank = jnp.sum(
        ((key[:, None] == key[None, :]) & (items[None, :] < items[:, None])).astype(jnp.int32), axis=1
    )
    is_key = key[:, None] == keys[None, :]
    even = (jnp.sum(is_key.astype(jnp.int32), axis=0) + 1) // 2 * 2
    near_key = keys < local_rows
    before = (keys[:, None] > keys[None, :]) & (near_key[:, None] == near_key[None, :])
    first = jnp.sum(jnp.where(before, even[None, :], 0), axis=1)
    pos = rank + jnp.sum(jnp.where(is_key, first[None, :], 0), axis=1)
    value = ((items << col_bits) | col) << index_bits | index
    empty = (local_rows << index_bits) | (2 * local_rows)

    def listed(chosen):
        pick = jnp.arange(length)[:, None] == jnp.where(chosen, pos, -1)[None, :]
        return empty + jnp.sum(jnp.where(pick, value[None, :] - empty, 0), axis=1)

    near_half = listed((key >= 0) & (key < local_rows))
    far_half = listed(key >= local_rows)
    near_count = jnp.sum(jnp.where(near_key, even, 0)).reshape(1)
    far_count = jnp.sum(jnp.where(near_key, 0, even)).reshape(1)
    return near_half, near_count, far_half, far_count


def add_blocks(first_sweep, room, list_ref, count_ref, blocks_ref, packed_ref, ext, acc, buf, sems, local_rows):
    index_bits, col_bits = bits_of(local_rows)
    width = buf.shape[-1]
    chunks = lax.div(count_ref[0] + (GROUP - 1), jnp.int32(GROUP))

    def copies(chunk):
        slot = lax.rem(chunk, BUFFERS)
        if not first_sweep:
            return [
                pltpu.make_async_copy(
                    packed_ref.at[pl.ds(chunk * GROUP * width, GROUP * width)], buf.at[slot], sems.at[slot, 0]
                )
            ]
        out = []
        for g in range(GROUP):
            item = list_ref[chunk * GROUP + g] >> (index_bits + col_bits)
            part = lax.div(item, jnp.int32(room))
            place = item - part * room
            out.append(
                pltpu.make_async_copy(
                    blocks_ref.at[part, pl.ds(pl.multiple_of(place * width, width), width)],
                    buf.at[slot, g * width : (g + 1) * width],
                    sems.at[slot, g],
                )
            )
        return out

    def write(chunk):
        slot = lax.rem(chunk, BUFFERS)
        return pltpu.make_async_copy(
            buf.at[slot], packed_ref.at[pl.ds(chunk * GROUP * width, GROUP * width)], sems.at[slot, GROUP]
        )

    def start(chunk):
        @pl.when(chunk < chunks)
        def _():
            for copy in copies(chunk):
                copy.start()

    for ahead in range(BUFFERS - 1):
        start(jnp.int32(ahead))

    def body(chunk, carry):
        if first_sweep:

            @pl.when(chunk > 0)
            def _():
                write(chunk - 1).wait()

        start(chunk + (BUFFERS - 1))
        for copy in copies(chunk):
            copy.wait()
        if first_sweep:
            write(chunk).start()
        slot = lax.rem(chunk, BUFFERS)
        mask = (1 << index_bits) - 1
        for g in range(0, GROUP, 2):
            item = list_ref[chunk * GROUP + g]
            other = list_ref[chunk * GROUP + g + 1]
            col = (item >> index_bits) & ((1 << col_bits) - 1)
            rows = jnp.concatenate([ext[item & mask], ext[other & mask]], axis=1)
            pair = buf[slot, g * width : (g + 2) * width]
            acc[col] += jnp.dot(rows, pair, preferred_element_type=jnp.float32)
        return carry

    lax.fori_loop(0, chunks, body, 0)
    if first_sweep:

        @pl.when(chunks > 0)
        def _():
            write(chunks - 1).wait()


def near_kernel(first_sweep, room, list_ref, count_ref, blocks_ref, own_ref, dir_ref, res_ref, *rest):
    if first_sweep:
        out_ref, packed_ref, ext, acc, buf, sems = rest
    else:
        out_ref, ext, acc, buf, sems = rest
        packed_ref = blocks_ref
    rows = dir_ref.shape[0]
    acc[0:rows] = res_ref[...] - dir_ref[...]
    ext[0:rows] = own_ref[...]
    ext[2 * rows] = jnp.zeros_like(ext[0])
    add_blocks(first_sweep, room, list_ref, count_ref, blocks_ref, packed_ref, ext, acc, buf, sems, rows)
    out_ref[...] = acc[0:rows]


def far_kernel(first_sweep, last, room, list_ref, count_ref, coef_ref, blocks_ref, low_ref, high_ref, part_ref, *rest):
    *refs, ext, acc, buf, sems, ext_sems = rest
    packed_ref = refs.pop() if first_sweep else blocks_ref
    if last:
        (res_out,) = refs
    else:
        dir_ref, adj_ref, res_out, dir_out, adj_out, round_out = refs
    rows = part_ref.shape[0]
    low = pltpu.make_async_copy(low_ref, ext.at[0:rows], ext_sems.at[0])
    high = pltpu.make_async_copy(high_ref, ext.at[rows : 2 * rows], ext_sems.at[1])
    low.start()
    high.start()
    acc[0:rows] = part_ref[...]
    ext[2 * rows] = jnp.zeros_like(part_ref[0]).astype(jnp.bfloat16)
    low.wait()
    high.wait()
    add_blocks(first_sweep, room, list_ref, count_ref, blocks_ref, packed_ref, ext, acc, buf, sems, rows)
    res = acc[0:rows]
    res_out[...] = res
    if not last:
        direction = coef_ref[0] * dir_ref[...] + coef_ref[1] * res
        dir_out[...] = direction
        adj_out[...] = adj_ref[...] + direction
        round_out[...] = direction.astype(jnp.bfloat16)


def local(
    factor_left,
    factor_right,
    state_diag,
    owner,
    col_local,
    row_shift,
    row_local,
    rhs_in,
    low_bound,
    high_bound,
):
    peers = lax.axis_size("rows")
    sides = lax.axis_size("rhs")
    slots = owner.shape[0]
    width = factor_left.shape[1]
    local_rows, columns, _ = rhs_in.shape
    room = min(slots, max(2, 3 * slots // peers))
    dest = owner[:, 0]

    scaled = (state_diag[:, :, None] * factor_right).astype(jnp.bfloat16)
    blocks = jnp.einsum(
        "kam,kmb->kab", factor_left, scaled, preferred_element_type=jnp.float32
    ).astype(jnp.bfloat16)
    index = row_local + jnp.where(row_shift == 2, local_rows, 0)
    near = (row_shift == 1).astype(jnp.int32)
    send = make_buckets(blocks, dest, col_local, index, near, peers, room)
    got = route(send, peers, sides)
    notes = got[:, room * width :, :].astype(jnp.int32)
    near_list, near_count, far_list, far_count = block_lists(notes, room, local_rows)
    packed_shape = jax.ShapeDtypeStruct((near_list.shape[0] * width, width), jnp.bfloat16)

    low = low_bound[0]
    high = high_bound[0]
    theta = (high + low) / 2.0
    delta = (high - low) / 2.0
    sigma = theta / delta
    rho = 1.0 / sigma
    residual = rhs_in
    direction = residual / theta
    adjoint = direction
    rounded = direction.astype(jnp.bfloat16)

    forward = [(i, (i + 1) % peers) for i in range(peers)]
    backward = [(i, (i - 1) % peers) for i in range(peers)]
    smem = pl.BlockSpec(memory_space=pltpu.SMEM)
    vmem = pl.BlockSpec(memory_space=pltpu.VMEM)
    hbm = pl.BlockSpec(memory_space=pltpu.HBM)
    anywhere = pl.BlockSpec(memory_space=pl.ANY)
    field = jax.ShapeDtypeStruct(rhs_in.shape, jnp.float32)
    work = [
        pltpu.VMEM((2 * local_rows + 1, columns, width), jnp.bfloat16),
        pltpu.VMEM((local_rows + 1, columns, width), jnp.float32),
        pltpu.VMEM((BUFFERS, GROUP * width, width), jnp.bfloat16),
        pltpu.SemaphoreType.DMA((BUFFERS, GROUP + 1)),
    ]
    params = pltpu.CompilerParams(vmem_limit_bytes=24 * 1024 * 1024)

    def cost(amount):
        return pl.CostEstimate(
            flops=2 * amount * columns * width * width,
            bytes_accessed=amount * width * width * 2 + 4 * rhs_in.size * 4,
            transcendentals=0,
        )

    near_blocks, far_blocks = got, got
    for sweep in range(ITERS):
        first_sweep, last = sweep == 0, sweep + 1 == ITERS
        low_rows = lax.ppermute(rounded, "rows", forward)
        high_rows = lax.ppermute(rounded, "rows", backward)
        result = pl.pallas_call(
            functools.partial(near_kernel, first_sweep, room),
            out_shape=[field] + [packed_shape] * first_sweep,
            in_specs=[smem, smem, hbm, vmem, vmem, vmem],
            out_specs=[vmem] + [hbm] * first_sweep,
            scratch_shapes=work,
            compiler_params=params,
            cost_estimate=cost(near_list.shape[0] // 4),
            name="near_first" if first_sweep else "near",
        )(near_list, near_count, near_blocks, rounded, direction, residual)
        part = result[0]
        if first_sweep:
            near_blocks = result[1]
        if last:
            coef = jnp.zeros((2,), jnp.float32)
        else:
            rho_next = 1.0 / (2.0 * sigma - rho)
            coef = jnp.stack([rho_next * rho, 2.0 * rho_next / delta])
            rho = rho_next
        fields = [] if last else [direction, adjoint]
        outs = [field] if last else [field] * 3 + [jax.ShapeDtypeStruct(rhs_in.shape, jnp.bfloat16)]
        result = pl.pallas_call(
            functools.partial(far_kernel, first_sweep, last, room),
            out_shape=outs + [packed_shape] * first_sweep,
            in_specs=[smem, smem, smem, hbm, anywhere, anywhere, vmem] + [vmem] * len(fields),
            out_specs=[vmem] * len(outs) + [hbm] * first_sweep,
            scratch_shapes=work + [pltpu.SemaphoreType.DMA((2,))],
            compiler_params=params,
            cost_estimate=cost(near_list.shape[0] // 2),
            name="far_last" if last else "far_first" if first_sweep else "far",
        )(far_list, far_count, coef, far_blocks, low_rows, high_rows, part, *fields)
        residual = result[0]
        if first_sweep:
            far_blocks = result[-1]
        if not last:
            direction, adjoint, rounded = result[1:4]
    return (adjoint, residual)


def solution(mesh):
    placed = (
        P(("rows", "rhs"), None, None),
        P(("rows", "rhs"), None, None),
        P(("rows", "rhs"), None),
        P(("rows", "rhs"), None),
        P(("rows", "rhs")),
        P(("rows", "rhs")),
        P(("rows", "rhs")),
        P("rows", "rhs", None),
        P(),
        P(),
    )
    return jax.shard_map(
        local,
        mesh=mesh,
        in_specs=placed,
        out_specs=(P("rows", "rhs", None), P("rows", "rhs", None)),
        check_vma=False,
    )
```

```python
import functools

import jax
import jax.numpy as jnp
from jax import lax
from jax.experimental import pallas as pl
from jax.experimental.pallas import tpu as pltpu
from jax.sharding import PartitionSpec as P

ITERS = 4
GROUP = 16
BUFFERS = 4
VMEM_LIMIT = 54 * 1024 * 1024
MESH = pl.DeviceIdType.MESH


def bits_of(local_rows):
    return (2 * local_rows).bit_length(), local_rows.bit_length()


def form_kernel(room, left_ref, right_ref, diag_ref, dest_ref, col_ref, shift_ref, row_ref, rows_ref, send_ref, notes, filled):
    slots, width, _ = left_ref.shape
    peers = send_ref.shape[0]
    notes[...] = jnp.zeros_like(notes)
    for owner in range(peers):
        filled[owner] = 0
    line = lax.broadcasted_iota(jnp.int32, notes.shape[1:], 0)
    lane = lax.broadcasted_iota(jnp.int32, notes.shape[1:], 1)
    for k in range(slots):
        scaled = (diag_ref[:, k : k + 1] * right_ref[k].astype(jnp.float32)).astype(jnp.bfloat16)
        block = jnp.dot(left_ref[k], scaled, preferred_element_type=jnp.float32)
        owner = dest_ref[k]
        place = filled[owner]
        filled[owner] = place + 1
        send_ref[owner, pl.ds(pl.multiple_of(place * width, width), width)] = block.astype(jnp.bfloat16)
        shift = shift_ref[k]
        index = row_ref[k] + jnp.where(shift == 2, rows_ref[0], 0)
        near = jnp.where(shift == 1, 1, 0)
        note = jnp.where(line == 0, 1, jnp.where(line == 1, col_ref[k], jnp.where(line == 2, index, near)))
        notes[owner] = jnp.where((lane == place) & (line < 4), note, notes[owner])
    for owner in range(peers):
        send_ref[owner, room * width : room * width + 16] = notes[owner].astype(jnp.float32).astype(jnp.bfloat16)


def form(left, right, diag, dest, col, shift, row, local_rows, peers, room):
    slots, width, _ = left.shape
    smem = pl.BlockSpec(memory_space=pltpu.SMEM)
    vmem = pl.BlockSpec(memory_space=pltpu.VMEM)
    return pl.pallas_call(
        functools.partial(form_kernel, room),
        out_shape=jax.ShapeDtypeStruct((peers, room * width + 16, width), jnp.bfloat16),
        in_specs=[vmem, vmem, vmem, smem, smem, smem, smem, smem],
        out_specs=vmem,
        scratch_shapes=[
            pltpu.VMEM((peers, 16, width), jnp.int32),
            pltpu.SMEM((peers,), jnp.int32),
        ],
        compiler_params=pltpu.CompilerParams(vmem_limit_bytes=VMEM_LIMIT),
        name="form",
    )(left, right, diag.T, dest, col, shift, row, jnp.full((1,), local_rows, jnp.int32))


def route_kernel(peers, sides, pieces, send_ref, got_ref, own_sem, send_sems, recv_sems):
    me, side = lax.axis_index("rows"), lax.axis_index("rhs")
    across, beside = side ^ 2, side ^ 1
    paired = peers & (peers - 1) == 0

    def target(d):
        return me ^ d if paired else lax.rem(me + d, peers)

    def source(d):
        return me ^ d if paired else lax.rem(me - d + peers, peers)

    barrier = pltpu.get_barrier_semaphore()
    for d in range(1, peers):
        pl.semaphore_signal(barrier, inc=1, device_id=(source(d), side), device_id_type=MESH)
    for other in (across, beside):
        pl.semaphore_signal(barrier, inc=1, device_id=(me, other), device_id_type=MESH)
    pl.semaphore_wait(barrier, peers + 1)

    def remote(kind, d, piece, src, slot, device):
        begin, end = pieces[piece]
        return pltpu.make_async_remote_copy(
            src_ref=src.at[begin:end],
            dst_ref=got_ref.at[slot, begin:end],
            send_sem=send_sems.at[kind, d, piece],
            recv_sem=recv_sems.at[kind, d, piece],
            device_id=device,
            device_id_type=MESH,
        )

    def to_owner(d, p):
        return remote(0, d, p, send_ref.at[target(d)], me * sides + side, (target(d), side))

    def held(d):
        return send_ref.at[me] if d == 0 else got_ref.at[source(d) * sides + side]

    def to_across(d, p):
        return remote(1, d, p, held(d), source(d) * sides + side, (me, across))

    def to_beside(d, p):
        return remote(2, d, p, held(d), source(d) * sides + side, (me, beside))

    def on_beside(d, p):
        slot = source(d) * sides + across
        return remote(3, d, p, got_ref.at[slot], slot, (me, beside))

    count = len(pieces)
    near = [(d, p) for d in range(1, peers // 2) for p in range(count)]
    far = [(d, p) for d in range(peers // 2, peers) for p in range(count)]
    follow = {}
    for queue in (near, far):
        follow.update(zip(queue, queue[2:]))
    for item in far[:2] + near[:2]:
        to_owner(*item).start()
    own = pltpu.make_async_copy(send_ref.at[me], got_ref.at[me * sides + side], own_sem)
    own.start()
    order = [(0, p) for p in range(count)]
    while near or far:
        order += near[:2] + far[:1]
        near, far = near[2:], far[1:]
    for step in range(len(order) + 2):
        if step < len(order):
            item = order[step]
            if item[0] > 0:
                to_owner(*item).wait_recv()
            to_across(*item).start()
            to_beside(*item).start()
            if item in follow:
                to_owner(*item).wait_send()
                to_owner(*follow[item]).start()
        if step >= 2:
            to_across(*order[step - 2]).wait_recv()
            on_beside(*order[step - 2]).start()
    own.wait()
    for item in order:
        if item[0] > 0 and item not in follow:
            to_owner(*item).wait_send()
        to_across(*item).wait_send()
        to_beside(*item).wait()
        on_beside(*item).wait()


def route(send, peers, sides, room):
    rows, width = send.shape[1:]
    if peers > 16 or room < 2:
        pieces = ((0, rows),)
    else:
        pieces = ((0, room // 2 * width), (room // 2 * width, rows))
    return pl.pallas_call(
        functools.partial(route_kernel, peers, sides, pieces),
        out_shape=jax.ShapeDtypeStruct((peers * sides, rows, width), send.dtype),
        in_specs=[pl.BlockSpec(memory_space=pltpu.HBM)],
        out_specs=pl.BlockSpec(memory_space=pltpu.HBM),
        scratch_shapes=[
            pltpu.SemaphoreType.DMA,
            pltpu.SemaphoreType.DMA((4, peers, len(pieces))),
            pltpu.SemaphoreType.DMA((4, peers, len(pieces))),
        ],
        compiler_params=pltpu.CompilerParams(collective_id=0, has_side_effects=True),
        name="route",
    )(send)


def block_lists(notes, room, local_rows):
    index_bits, col_bits = bits_of(local_rows)
    filled, col, index, near = [notes[:, i, :room].reshape(-1) for i in range(4)]
    count = filled.shape[0]
    length = -(-(count + 2 * local_rows) // GROUP) * GROUP
    key = jnp.where(filled == 1, (1 - near) * local_rows + col, -1)
    items = jnp.arange(count)
    keys = jnp.arange(2 * local_rows)
    rank = jnp.sum(
        ((key[:, None] == key[None, :]) & (items[None, :] < items[:, None])).astype(jnp.int32), axis=1
    )
    is_key = key[:, None] == keys[None, :]
    even = (jnp.sum(is_key.astype(jnp.int32), axis=0) + 1) // 2 * 2
    near_key = keys < local_rows
    before = (keys[:, None] > keys[None, :]) & (near_key[:, None] == near_key[None, :])
    first = jnp.sum(jnp.where(before, even[None, :], 0), axis=1)
    pos = rank + jnp.sum(jnp.where(is_key, first[None, :], 0), axis=1)
    value = ((items << col_bits) | col) << index_bits | index
    some = jnp.max(jnp.where(filled == 1, items, 0))
    empty = ((some << col_bits) | local_rows) << index_bits | (2 * local_rows)

    def listed(chosen):
        pick = jnp.arange(length)[:, None] == jnp.where(chosen, pos, -1)[None, :]
        return empty + jnp.sum(jnp.where(pick, value[None, :] - empty, 0), axis=1)

    near_half = listed((key >= 0) & (key < local_rows))
    far_half = listed(key >= local_rows)
    near_count = jnp.sum(jnp.where(near_key, even, 0)).reshape(1)
    far_count = jnp.sum(jnp.where(near_key, 0, even)).reshape(1)
    return near_half, near_count, far_half, far_count


def add_blocks(first_sweep, room, list_ref, count_ref, blocks_ref, packed_ref, ext, acc, buf, sems, local_rows):
    index_bits, col_bits = bits_of(local_rows)
    width = buf.shape[-1]
    chunks = lax.div(count_ref[0] + (GROUP - 1), jnp.int32(GROUP))

    def copies(chunk):
        slot = lax.rem(chunk, BUFFERS)
        if not first_sweep:
            return [
                pltpu.make_async_copy(
                    packed_ref.at[pl.ds(chunk * GROUP * width, GROUP * width)], buf.at[slot], sems.at[slot, 0]
                )
            ]
        out = []
        for g in range(GROUP):
            item = list_ref[chunk * GROUP + g] >> (index_bits + col_bits)
            part = lax.div(item, jnp.int32(room))
            place = item - part * room
            out.append(
                pltpu.make_async_copy(
                    blocks_ref.at[part, pl.ds(pl.multiple_of(place * width, width), width)],
                    buf.at[slot, g * width : (g + 1) * width],
                    sems.at[slot, g],
                )
            )
        return out

    def write(chunk):
        slot = lax.rem(chunk, BUFFERS)
        return pltpu.make_async_copy(
            buf.at[slot], packed_ref.at[pl.ds(chunk * GROUP * width, GROUP * width)], sems.at[slot, GROUP]
        )

    def start(chunk):
        @pl.when(chunk < chunks)
        def _():
            for copy in copies(chunk):
                copy.start()

    for ahead in range(BUFFERS - 1):
        start(jnp.int32(ahead))

    def body(chunk, carry):
        if first_sweep:

            @pl.when(chunk > 0)
            def _():
                write(chunk - 1).wait()

        start(chunk + (BUFFERS - 1))
        for copy in copies(chunk):
            copy.wait()
        if first_sweep:
            write(chunk).start()
        slot = lax.rem(chunk, BUFFERS)
        mask = (1 << index_bits) - 1
        for g in range(0, GROUP, 2):
            item = list_ref[chunk * GROUP + g]
            other = list_ref[chunk * GROUP + g + 1]
            col = (item >> index_bits) & ((1 << col_bits) - 1)
            rows = jnp.concatenate([ext[item & mask], ext[other & mask]], axis=1)
            pair = buf[slot, g * width : (g + 2) * width]
            acc[col] += jnp.dot(rows, pair, preferred_element_type=jnp.float32)
        return carry

    lax.fori_loop(0, chunks, body, 0)
    if first_sweep:

        @pl.when(chunks > 0)
        def _():
            write(chunks - 1).wait()


def near_kernel(first_sweep, room, list_ref, count_ref, blocks_ref, own_ref, dir_ref, res_ref, *rest):
    if first_sweep:
        out_ref, packed_ref, ext, acc, buf, sems = rest
    else:
        out_ref, ext, acc, buf, sems = rest
        packed_ref = blocks_ref
    rows = dir_ref.shape[0]
    acc[0:rows] = res_ref[...] - dir_ref[...]
    ext[0:rows] = own_ref[...]
    ext[2 * rows] = jnp.zeros_like(ext[0])
    add_blocks(first_sweep, room, list_ref, count_ref, blocks_ref, packed_ref, ext, acc, buf, sems, rows)
    out_ref[...] = acc[0:rows]


def far_kernel(first_sweep, last, room, list_ref, count_ref, coef_ref, blocks_ref, low_ref, high_ref, part_ref, *rest):
    *refs, ext, acc, buf, sems, ext_sems = rest
    packed_ref = refs.pop() if first_sweep else blocks_ref
    if last:
        (res_out,) = refs
    else:
        dir_ref, adj_ref, res_out, dir_out, adj_out, round_out = refs
    rows = part_ref.shape[0]
    low = pltpu.make_async_copy(low_ref, ext.at[0:rows], ext_sems.at[0])
    high = pltpu.make_async_copy(high_ref, ext.at[rows : 2 * rows], ext_sems.at[1])
    low.start()
    high.start()
    acc[0:rows] = part_ref[...]
    ext[2 * rows] = jnp.zeros_like(part_ref[0]).astype(jnp.bfloat16)
    low.wait()
    high.wait()
    add_blocks(first_sweep, room, list_ref, count_ref, blocks_ref, packed_ref, ext, acc, buf, sems, rows)
    res = acc[0:rows]
    res_out[...] = res
    if not last:
        direction = coef_ref[0] * dir_ref[...] + coef_ref[1] * res
        dir_out[...] = direction
        adj_out[...] = adj_ref[...] + direction
        round_out[...] = direction.astype(jnp.bfloat16)


def local(
    factor_left,
    factor_right,
    state_diag,
    owner,
    col_local,
    row_shift,
    row_local,
    rhs_in,
    low_bound,
    high_bound,
):
    peers = lax.axis_size("rows")
    sides = lax.axis_size("rhs")
    slots = owner.shape[0]
    width = factor_left.shape[1]
    local_rows, columns, _ = rhs_in.shape
    room = min(slots, max(2, 3 * slots // peers))
    dest = owner[:, 0]

    send = form(
        factor_left, factor_right, state_diag, dest, col_local, row_shift, row_local, local_rows, peers, room
    )
    got = route(send, peers, sides, room)
    notes = got[:, room * width :, :].astype(jnp.int32)
    near_list, near_count, far_list, far_count = block_lists(notes, room, local_rows)
    packed_shape = jax.ShapeDtypeStruct((near_list.shape[0] * width, width), jnp.bfloat16)

    low = low_bound[0]
    high = high_bound[0]
    theta = (high + low) / 2.0
    delta = (high - low) / 2.0
    sigma = theta / delta
    rho = 1.0 / sigma
    residual = rhs_in
    direction = residual / theta
    adjoint = direction
    rounded = direction.astype(jnp.bfloat16)

    forward = [(i, (i + 1) % peers) for i in range(peers)]
    backward = [(i, (i - 1) % peers) for i in range(peers)]
    smem = pl.BlockSpec(memory_space=pltpu.SMEM)
    vmem = pl.BlockSpec(memory_space=pltpu.VMEM)
    hbm = pl.BlockSpec(memory_space=pltpu.HBM)
    anywhere = pl.BlockSpec(memory_space=pl.ANY)
    field = jax.ShapeDtypeStruct(rhs_in.shape, jnp.float32)
    work = [
        pltpu.VMEM((2 * local_rows + 1, columns, width), jnp.bfloat16),
        pltpu.VMEM((local_rows + 1, columns, width), jnp.float32),
        pltpu.VMEM((BUFFERS, GROUP * width, width), jnp.bfloat16),
        pltpu.SemaphoreType.DMA((BUFFERS, GROUP + 1)),
    ]
    params = pltpu.CompilerParams(vmem_limit_bytes=VMEM_LIMIT)

    def cost(amount):
        return pl.CostEstimate(
            flops=2 * amount * columns * width * width,
            bytes_accessed=amount * width * width * 2 + 4 * rhs_in.size * 4,
            transcendentals=0,
        )

    near_blocks, far_blocks = got, got
    for sweep in range(ITERS):
        first_sweep, last = sweep == 0, sweep + 1 == ITERS
        low_rows = lax.ppermute(rounded, "rows", forward)
        high_rows = lax.ppermute(rounded, "rows", backward)
        result = pl.pallas_call(
            functools.partial(near_kernel, first_sweep, room),
            out_shape=[field] + [packed_shape] * first_sweep,
            in_specs=[smem, smem, hbm, vmem, vmem, vmem],
            out_specs=[vmem] + [hbm] * first_sweep,
            scratch_shapes=work,
            compiler_params=params,
            cost_estimate=cost(near_list.shape[0] // 4),
            name="near_first" if first_sweep else "near",
        )(near_list, near_count, near_blocks, rounded, direction, residual)
        part = result[0]
        if first_sweep:
            near_blocks = result[1]
        if last:
            coef = jnp.zeros((2,), jnp.float32)
        else:
            rho_next = 1.0 / (2.0 * sigma - rho)
            coef = jnp.stack([rho_next * rho, 2.0 * rho_next / delta])
            rho = rho_next
        fields = [] if last else [direction, adjoint]
        outs = [field] if last else [field] * 3 + [jax.ShapeDtypeStruct(rhs_in.shape, jnp.bfloat16)]
        result = pl.pallas_call(
            functools.partial(far_kernel, first_sweep, last, room),
            out_shape=outs + [packed_shape] * first_sweep,
            in_specs=[smem, smem, smem, hbm, anywhere, anywhere, vmem] + [vmem] * len(fields),
            out_specs=[vmem] * len(outs) + [hbm] * first_sweep,
            scratch_shapes=work + [pltpu.SemaphoreType.DMA((2,))],
            compiler_params=params,
            cost_estimate=cost(near_list.shape[0] // 2),
            name="far_last" if last else "far_first" if first_sweep else "far",
        )(far_list, far_count, coef, far_blocks, low_rows, high_rows, part, *fields)
        residual = result[0]
        if first_sweep:
            far_blocks = result[-1]
        if not last:
            direction, adjoint, rounded = result[1:4]
    return (adjoint, residual)


def solution(mesh):
    placed = (
        P(("rows", "rhs"), None, None),
        P(("rows", "rhs"), None, None),
        P(("rows", "rhs"), None),
        P(("rows", "rhs"), None),
        P(("rows", "rhs")),
        P(("rows", "rhs")),
        P(("rows", "rhs")),
        P("rows", "rhs", None),
        P(),
        P(),
    )
    return jax.shard_map(
        local,
        mesh=mesh,
        in_specs=placed,
        out_specs=(P("rows", "rhs", None), P("rows", "rhs", None)),
        check_vma=False,
    )
```

```python
import functools

import jax
import jax.numpy as jnp
from jax import lax
from jax.experimental import pallas as pl
from jax.experimental.pallas import tpu as pltpu
from jax.sharding import PartitionSpec as P

ITERS = 4
GROUP = 16
BUFFERS = 4
BATCH = 4
VMEM_LIMIT = 40 * 1024 * 1024
SPARE = 2
MESH = pl.DeviceIdType.MESH


def bits_of(local_rows):
    return (2 * local_rows).bit_length(), local_rows.bit_length()


def form_kernel(room, left_ref, right_ref, diag_ref, dest_ref, col_ref, shift_ref, row_ref, rows_ref, send_ref, notes, filled):
    slots, width, _ = left_ref.shape
    peers = send_ref.shape[0]
    notes[...] = jnp.zeros_like(notes)
    for owner in range(peers):
        filled[owner] = 0
    line = lax.broadcasted_iota(jnp.int32, notes.shape[1:], 0)
    lane = lax.broadcasted_iota(jnp.int32, notes.shape[1:], 1)
    for k in range(slots):
        scaled = (diag_ref[:, k : k + 1] * right_ref[k].astype(jnp.float32)).astype(jnp.bfloat16)
        block = jnp.dot(left_ref[k], scaled, preferred_element_type=jnp.float32)
        owner = dest_ref[k]
        place = filled[owner]
        filled[owner] = place + 1
        send_ref[owner, pl.ds(pl.multiple_of(place * width, width), width)] = block.astype(jnp.bfloat16)
        shift = shift_ref[k]
        index = row_ref[k] + jnp.where(shift == 2, rows_ref[0], 0)
        near = jnp.where(shift == 1, 1, 0)
        note = jnp.where(line == 0, 1, jnp.where(line == 1, col_ref[k], jnp.where(line == 2, index, near)))
        notes[owner] = jnp.where((lane == place) & (line < 4), note, notes[owner])
    for owner in range(peers):
        send_ref[owner, room * width : room * width + 16] = notes[owner].astype(jnp.float32).astype(jnp.bfloat16)


def form(left, right, diag, dest, col, shift, row, local_rows, peers, room):
    slots, width, _ = left.shape
    smem = pl.BlockSpec(memory_space=pltpu.SMEM)
    vmem = pl.BlockSpec(memory_space=pltpu.VMEM)
    return pl.pallas_call(
        functools.partial(form_kernel, room),
        out_shape=jax.ShapeDtypeStruct((peers, room * width + 16, width), jnp.bfloat16),
        in_specs=[vmem, vmem, vmem, smem, smem, smem, smem, smem],
        out_specs=vmem,
        scratch_shapes=[
            pltpu.VMEM((peers, 16, width), jnp.int32),
            pltpu.SMEM((peers,), jnp.int32),
        ],
        compiler_params=pltpu.CompilerParams(vmem_limit_bytes=VMEM_LIMIT),
        name="form",
    )(left, right, diag.T, dest, col, shift, row, jnp.full((1,), local_rows, jnp.int32))


def route_kernel(
    peers, sides, pieces, send_ref, field_ref, got_ref, low_ref, high_ref, own_sem, send_sems, recv_sems, halo_sends, halo_recvs
):
    me, side = lax.axis_index("rows"), lax.axis_index("rhs")
    across, beside = side ^ 2, side ^ 1
    paired = peers & (peers - 1) == 0

    def target(d):
        return me ^ d if paired else lax.rem(me + d, peers)

    def source(d):
        return me ^ d if paired else lax.rem(me - d + peers, peers)

    barrier = pltpu.get_barrier_semaphore()
    for d in range(1, peers):
        pl.semaphore_signal(barrier, inc=1, device_id=(source(d), side), device_id_type=MESH)
    for other in (across, beside):
        pl.semaphore_signal(barrier, inc=1, device_id=(me, other), device_id_type=MESH)
    pl.semaphore_wait(barrier, peers + 1)

    def remote(kind, d, piece, src, slot, device):
        begin, end = pieces[piece]
        return pltpu.make_async_remote_copy(
            src_ref=src.at[begin:end],
            dst_ref=got_ref.at[slot, begin:end],
            send_sem=send_sems.at[kind, d, piece],
            recv_sem=recv_sems.at[kind, d, piece],
            device_id=device,
            device_id_type=MESH,
        )

    def to_owner(d, p):
        return remote(0, d, p, send_ref.at[target(d)], me * sides + side, (target(d), side))

    def held(d):
        return send_ref.at[me] if d == 0 else got_ref.at[source(d) * sides + side]

    def to_across(d, p):
        return remote(1, d, p, held(d), source(d) * sides + side, (me, across))

    def to_beside(d, p):
        return remote(2, d, p, held(d), source(d) * sides + side, (me, beside))

    def on_beside(d, p):
        slot = source(d) * sides + across
        return remote(3, d, p, got_ref.at[slot], slot, (me, beside))

    count = len(pieces)
    near = [(d, p) for d in range(1, peers // 2) for p in range(count)]
    far = [(d, p) for d in range(peers // 2, peers) for p in range(count)]
    follow = {}
    for queue in (near, far):
        follow.update(zip(queue, queue[2:]))
    for item in far[:2] + near[:2]:
        to_owner(*item).start()

    def halo(end, ref, step):
        return pltpu.make_async_remote_copy(
            src_ref=field_ref,
            dst_ref=ref,
            send_sem=halo_sends.at[end],
            recv_sem=halo_recvs.at[end],
            device_id=(lax.rem(me + step, peers), side),
            device_id_type=MESH,
        )

    halos = [halo(0, low_ref, 1), halo(1, high_ref, peers - 1)]
    for copy in halos:
        copy.start()
    own = pltpu.make_async_copy(send_ref.at[me], got_ref.at[me * sides + side], own_sem)
    own.start()
    order = [(0, p) for p in range(count)]
    while near or far:
        order += near[:2] + far[:1]
        near, far = near[2:], far[1:]
    for step in range(len(order) + 2):
        if step < len(order):
            item = order[step]
            if item[0] > 0:
                to_owner(*item).wait_recv()
            to_across(*item).start()
            to_beside(*item).start()
            if item in follow:
                to_owner(*item).wait_send()
                to_owner(*follow[item]).start()
        if step >= 2:
            to_across(*order[step - 2]).wait_recv()
            on_beside(*order[step - 2]).start()
    own.wait()
    for copy in halos:
        copy.wait()
    for item in order:
        if item[0] > 0 and item not in follow:
            to_owner(*item).wait_send()
        to_across(*item).wait_send()
        to_beside(*item).wait()
        on_beside(*item).wait()


def route(send, field, peers, sides, room):
    rows, width = send.shape[1:]
    if peers > 16 or room < 2:
        pieces = ((0, rows),)
    else:
        pieces = ((0, room // 2 * width), (room // 2 * width, rows))
    return pl.pallas_call(
        functools.partial(route_kernel, peers, sides, pieces),
        out_shape=[
            jax.ShapeDtypeStruct((SPARE * peers * sides, rows, width), send.dtype),
            jax.ShapeDtypeStruct(field.shape, field.dtype),
            jax.ShapeDtypeStruct(field.shape, field.dtype),
        ],
        in_specs=[pl.BlockSpec(memory_space=pltpu.HBM)] * 2,
        out_specs=[pl.BlockSpec(memory_space=pltpu.HBM)] * 3,
        scratch_shapes=[
            pltpu.SemaphoreType.DMA,
            pltpu.SemaphoreType.DMA((4, peers, len(pieces))),
            pltpu.SemaphoreType.DMA((4, peers, len(pieces))),
            pltpu.SemaphoreType.DMA((2,)),
            pltpu.SemaphoreType.DMA((2,)),
        ],
        compiler_params=pltpu.CompilerParams(collective_id=0, has_side_effects=True),
        name="route",
    )(send, field)


def block_lists(notes, room, local_rows):
    index_bits, col_bits = bits_of(local_rows)
    filled, col, index, near = [notes[:, i, :room].reshape(-1) for i in range(4)]
    count = filled.shape[0]
    length = -(-(count + 2 * local_rows) // GROUP) * GROUP
    key = jnp.where(filled == 1, (1 - near) * local_rows + col, -1)
    items = jnp.arange(count)
    keys = jnp.arange(2 * local_rows)
    rank = jnp.sum(
        ((key[:, None] == key[None, :]) & (items[None, :] < items[:, None])).astype(jnp.int32), axis=1
    )
    is_key = key[:, None] == keys[None, :]
    even = (jnp.sum(is_key.astype(jnp.int32), axis=0) + 1) // 2 * 2
    near_key = keys < local_rows
    before = (keys[:, None] > keys[None, :]) & (near_key[:, None] == near_key[None, :])
    first = jnp.sum(jnp.where(before, even[None, :], 0), axis=1)
    pos = rank + jnp.sum(jnp.where(is_key, first[None, :], 0), axis=1)
    value = ((items << col_bits) | col) << index_bits | index
    some = jnp.max(jnp.where(filled == 1, items, 0))
    empty = ((some << col_bits) | local_rows) << index_bits | (2 * local_rows)

    def listed(chosen):
        pick = jnp.arange(length)[:, None] == jnp.where(chosen, pos, -1)[None, :]
        return empty + jnp.sum(jnp.where(pick, value[None, :] - empty, 0), axis=1)

    near_half = listed((key >= 0) & (key < local_rows))
    far_half = listed(key >= local_rows)
    near_count = jnp.sum(jnp.where(near_key, even, 0)).reshape(1)
    far_count = jnp.sum(jnp.where(near_key, 0, even)).reshape(1)
    return near_half, near_count, far_half, far_count


def add_blocks(first_sweep, room, list_ref, count_ref, blocks_ref, packed_ref, ext, acc, buf, sems, local_rows):
    index_bits, col_bits = bits_of(local_rows)
    width = buf.shape[-1]
    chunks = lax.div(count_ref[0] + (GROUP - 1), jnp.int32(GROUP))

    def whole(chunk):
        slot = lax.rem(chunk, BUFFERS)
        return pltpu.make_async_copy(
            packed_ref.at[pl.ds(chunk * GROUP * width, GROUP * width)], buf.at[slot], sems.at[slot, 0]
        )

    def copies(chunk):
        if not first_sweep:
            return [whole(chunk)]
        slot = lax.rem(chunk, BUFFERS)
        out = []
        for g in range(GROUP):
            item = list_ref[chunk * GROUP + g] >> (index_bits + col_bits)
            part = lax.div(item, jnp.int32(room))
            place = item - part * room
            out.append(
                pltpu.make_async_copy(
                    blocks_ref.at[part, pl.ds(pl.multiple_of(place * width, width), width)],
                    buf.at[slot, g * width : (g + 1) * width],
                    sems.at[slot, 0],
                )
            )
        return out

    def write(chunk):
        slot = lax.rem(chunk, BUFFERS)
        return pltpu.make_async_copy(
            buf.at[slot], packed_ref.at[pl.ds(chunk * GROUP * width, GROUP * width)], sems.at[slot, 1]
        )

    def start(chunk):
        @pl.when(chunk < chunks)
        def _():
            for copy in copies(chunk):
                copy.start()

    for ahead in range(BUFFERS - 1):
        start(jnp.int32(ahead))

    def body(chunk, carry):
        if first_sweep:

            @pl.when(chunk > 0)
            def _():
                write(chunk - 1).wait()

        start(chunk + (BUFFERS - 1))
        whole(chunk).wait()
        if first_sweep:
            write(chunk).start()
        slot = lax.rem(chunk, BUFFERS)
        mask = (1 << index_bits) - 1
        for begin in range(0, GROUP, 2 * BATCH):
            products = []
            for g in range(begin, begin + 2 * BATCH, 2):
                item = list_ref[chunk * GROUP + g]
                other = list_ref[chunk * GROUP + g + 1]
                rows = jnp.concatenate([ext[item & mask], ext[other & mask]], axis=1)
                pair = buf[slot, g * width : (g + 2) * width]
                col = (item >> index_bits) & ((1 << col_bits) - 1)
                products.append((col, jnp.dot(rows, pair, preferred_element_type=jnp.float32)))
            for col, product in products:
                acc[col] += product
        return carry

    lax.fori_loop(0, chunks, body, 0)
    if first_sweep:

        @pl.when(chunks > 0)
        def _():
            write(chunks - 1).wait()


def near_kernel(first_sweep, room, list_ref, count_ref, blocks_ref, own_ref, dir_ref, res_ref, *rest):
    if first_sweep:
        out_ref, packed_ref, ext, acc, buf, sems = rest
    else:
        out_ref, ext, acc, buf, sems = rest
        packed_ref = blocks_ref
    rows = dir_ref.shape[0]
    acc[0:rows] = res_ref[...] - dir_ref[...]
    ext[0:rows] = own_ref[...]
    ext[2 * rows] = jnp.zeros_like(ext[0])
    add_blocks(first_sweep, room, list_ref, count_ref, blocks_ref, packed_ref, ext, acc, buf, sems, rows)
    out_ref[...] = acc[0:rows]


def far_kernel(sweep, room, list_ref, count_ref, coef_ref, blocks_ref, low_ref, high_ref, part_ref, *rest):
    first_sweep, last = sweep == 0, sweep + 1 == ITERS
    *refs, ext, acc, buf, sems = rest
    packed_ref = refs.pop() if first_sweep else blocks_ref
    if last:
        (res_out,) = refs
    else:
        dir_ref, adj_ref, res_out, dir_out, adj_out, round_out = refs
    rows = part_ref.shape[0]
    acc[0:rows] = part_ref[...]
    ext[0:rows] = low_ref[...]
    ext[rows : 2 * rows] = high_ref[...]
    ext[2 * rows] = jnp.zeros_like(ext[0])
    add_blocks(first_sweep, room, list_ref, count_ref, blocks_ref, packed_ref, ext, acc, buf, sems, rows)
    res = acc[0:rows]
    res_out[...] = res
    if not last:
        direction = coef_ref[2 * sweep] * dir_ref[...] + coef_ref[2 * sweep + 1] * res
        dir_out[...] = direction
        adj_out[...] = adj_ref[...] + direction
        round_out[...] = direction.astype(jnp.bfloat16)


def local(
    factor_left,
    factor_right,
    state_diag,
    owner,
    col_local,
    row_shift,
    row_local,
    rhs_in,
    low_bound,
    high_bound,
):
    peers = lax.axis_size("rows")
    sides = lax.axis_size("rhs")
    slots = owner.shape[0]
    width = factor_left.shape[1]
    local_rows, columns, _ = rhs_in.shape
    room = min(slots, max(2, 3 * slots // peers))
    dest = owner[:, 0]

    send = form(
        factor_left, factor_right, state_diag, dest, col_local, row_shift, row_local, local_rows, peers, room
    )
    rounded = (rhs_in / ((high_bound[0] + low_bound[0]) / 2.0)).astype(jnp.bfloat16)
    got, low_rows, high_rows = route(send, rounded, peers, sides, room)
    notes = got[: peers * sides, room * width :, :].astype(jnp.int32)
    near_list, near_count, far_list, far_count = block_lists(notes, room, local_rows)
    packed_shape = jax.ShapeDtypeStruct((SPARE * near_list.shape[0] * width, width), jnp.bfloat16)

    low = low_bound[0]
    high = high_bound[0]
    theta = (high + low) / 2.0
    delta = (high - low) / 2.0
    sigma = theta / delta
    rho = 1.0 / sigma
    residual = rhs_in
    direction = residual / theta
    adjoint = direction
    coefs = []
    for _ in range(ITERS - 1):
        rho_next = 1.0 / (2.0 * sigma - rho)
        coefs += [rho_next * rho, 2.0 * rho_next / delta]
        rho = rho_next
    coefs = jnp.stack(coefs)

    forward = [(i, (i + 1) % peers) for i in range(peers)]
    backward = [(i, (i - 1) % peers) for i in range(peers)]
    smem = pl.BlockSpec(memory_space=pltpu.SMEM)
    vmem = pl.BlockSpec(memory_space=pltpu.VMEM)
    hbm = pl.BlockSpec(memory_space=pltpu.HBM)
    field = jax.ShapeDtypeStruct(rhs_in.shape, jnp.float32)
    work = [
        pltpu.VMEM((2 * local_rows + 1, columns, width), jnp.bfloat16),
        pltpu.VMEM((local_rows + 1, columns, width), jnp.float32),
        pltpu.VMEM((BUFFERS, GROUP * width, width), jnp.bfloat16),
        pltpu.SemaphoreType.DMA((BUFFERS, 2)),
    ]
    params = pltpu.CompilerParams(vmem_limit_bytes=VMEM_LIMIT)

    def cost(amount):
        return pl.CostEstimate(
            flops=2 * amount * columns * width * width,
            bytes_accessed=amount * width * width * 2 + 4 * rhs_in.size * 4,
            transcendentals=0,
        )

    near_blocks, far_blocks = got, got
    for sweep in range(ITERS):
        first_sweep, last = sweep == 0, sweep + 1 == ITERS
        if not first_sweep:
            low_rows = lax.ppermute(rounded, "rows", forward)
            high_rows = lax.ppermute(rounded, "rows", backward)
        result = pl.pallas_call(
            functools.partial(near_kernel, first_sweep, room),
            out_shape=[field] + [packed_shape] * first_sweep,
            in_specs=[smem, smem, hbm, vmem, vmem, vmem],
            out_specs=[vmem] + [hbm] * first_sweep,
            scratch_shapes=work,
            compiler_params=params,
            cost_estimate=cost(near_list.shape[0] // 4),
            name="near_first" if first_sweep else "near",
        )(near_list, near_count, near_blocks, rounded, direction, residual)
        part = result[0]
        if first_sweep:
            near_blocks = result[1]
        fields = [] if last else [direction, adjoint]
        outs = [field] if last else [field] * 3 + [jax.ShapeDtypeStruct(rhs_in.shape, jnp.bfloat16)]
        result = pl.pallas_call(
            functools.partial(far_kernel, sweep, room),
            out_shape=outs + [packed_shape] * first_sweep,
            in_specs=[smem, smem, smem, hbm, vmem, vmem, vmem] + [vmem] * len(fields),
            out_specs=[vmem] * len(outs) + [hbm] * first_sweep,
            scratch_shapes=work,
            compiler_params=params,
            cost_estimate=cost(near_list.shape[0] // 2),
            name="far_last" if last else "far_first" if first_sweep else "far",
        )(far_list, far_count, coefs, far_blocks, low_rows, high_rows, part, *fields)
        residual = result[0]
        if first_sweep:
            far_blocks = result[-1]
        if not last:
            direction, adjoint, rounded = result[1:4]
    return (adjoint, residual)


def solution(mesh):
    placed = (
        P(("rows", "rhs"), None, None),
        P(("rows", "rhs"), None, None),
        P(("rows", "rhs"), None),
        P(("rows", "rhs"), None),
        P(("rows", "rhs")),
        P(("rows", "rhs")),
        P(("rows", "rhs")),
        P("rows", "rhs", None),
        P(),
        P(),
    )
    return jax.shard_map(
        local,
        mesh=mesh,
        in_specs=placed,
        out_specs=(P("rows", "rhs", None), P("rows", "rhs", None)),
        check_vma=False,
    )
```

```python
import functools

import jax
import jax.numpy as jnp
from jax import lax
from jax.experimental import pallas as pl
from jax.experimental.pallas import tpu as pltpu
from jax.sharding import PartitionSpec as P

ITERS = 4
GROUP = 16
BUFFERS = 4
BATCH = 4
VMEM_LIMIT = 40 * 1024 * 1024
SPARE = 2
MESH = pl.DeviceIdType.MESH


def bits_of(local_rows):
    return (3 * local_rows).bit_length(), local_rows.bit_length()


def form_kernel(room, left_ref, right_ref, diag_ref, place_ref, send_ref, notes, filled):
    slots, width, _ = left_ref.shape
    peers = send_ref.shape[0]
    notes[...] = jnp.zeros_like(notes)
    for owner in range(peers):
        filled[owner] = 0
    line = lax.broadcasted_iota(jnp.int32, notes.shape[1:], 0)
    lane = lax.broadcasted_iota(jnp.int32, notes.shape[1:], 1)
    for k in range(slots):
        scaled = (diag_ref[:, k : k + 1] * right_ref[k].astype(jnp.float32)).astype(jnp.bfloat16)
        block = jnp.dot(left_ref[k], scaled, preferred_element_type=jnp.float32)
        owner = place_ref[k]
        place = filled[owner]
        filled[owner] = place + 1
        send_ref[owner, pl.ds(pl.multiple_of(place * width, width), width)] = block.astype(jnp.bfloat16)
        col, index = place_ref[slots + k], place_ref[2 * slots + k]
        note = jnp.where(line == 0, 1, jnp.where(line == 1, col, index))
        notes[owner] = jnp.where((lane == place) & (line < 3), note, notes[owner])
    for owner in range(peers):
        send_ref[owner, room * width : room * width + 16] = notes[owner].astype(jnp.float32).astype(jnp.bfloat16)


def form(left, right, diag, places, peers, room):
    slots, width, _ = left.shape
    smem = pl.BlockSpec(memory_space=pltpu.SMEM)
    vmem = pl.BlockSpec(memory_space=pltpu.VMEM)
    return pl.pallas_call(
        functools.partial(form_kernel, room),
        out_shape=jax.ShapeDtypeStruct((peers, room * width + 16, width), jnp.bfloat16),
        in_specs=[vmem, vmem, vmem, smem],
        out_specs=vmem,
        scratch_shapes=[
            pltpu.VMEM((peers, 16, width), jnp.int32),
            pltpu.SMEM((peers,), jnp.int32),
        ],
        compiler_params=pltpu.CompilerParams(vmem_limit_bytes=VMEM_LIMIT),
        name="form",
    )(left, right, diag.T, places)


def route_kernel(
    peers, sides, pieces, send_ref, field_ref, got_ref, low_ref, high_ref, own_sem, send_sems, recv_sems, halo_sends, halo_recvs
):
    me, side = lax.axis_index("rows"), lax.axis_index("rhs")
    across, beside = side ^ 2, side ^ 1
    paired = peers & (peers - 1) == 0

    def target(d):
        return me ^ d if paired else lax.rem(me + d, peers)

    def source(d):
        return me ^ d if paired else lax.rem(me - d + peers, peers)

    barrier = pltpu.get_barrier_semaphore()
    for d in range(1, peers):
        pl.semaphore_signal(barrier, inc=1, device_id=(source(d), side), device_id_type=MESH)
    for other in (across, beside):
        pl.semaphore_signal(barrier, inc=1, device_id=(me, other), device_id_type=MESH)
    pl.semaphore_wait(barrier, peers + 1)

    def remote(kind, d, piece, src, slot, device):
        begin, end = pieces[piece]
        return pltpu.make_async_remote_copy(
            src_ref=src.at[begin:end],
            dst_ref=got_ref.at[slot, begin:end],
            send_sem=send_sems.at[kind, d, piece],
            recv_sem=recv_sems.at[kind, d, piece],
            device_id=device,
            device_id_type=MESH,
        )

    def to_owner(d, p):
        return remote(0, d, p, send_ref.at[target(d)], me * sides + side, (target(d), side))

    def held(d):
        return send_ref.at[me] if d == 0 else got_ref.at[source(d) * sides + side]

    def to_across(d, p):
        return remote(1, d, p, held(d), source(d) * sides + side, (me, across))

    def to_beside(d, p):
        return remote(2, d, p, held(d), source(d) * sides + side, (me, beside))

    def on_beside(d, p):
        slot = source(d) * sides + across
        return remote(3, d, p, got_ref.at[slot], slot, (me, beside))

    count = len(pieces)
    near = [(d, p) for d in range(1, peers // 2) for p in range(count)]
    far = [(d, p) for d in range(peers // 2, peers) for p in range(count)]
    follow = {}
    for queue in (near, far):
        follow.update(zip(queue, queue[2:]))
    for item in far[:2] + near[:2]:
        to_owner(*item).start()

    def halo(end, ref, step):
        return pltpu.make_async_remote_copy(
            src_ref=field_ref,
            dst_ref=ref,
            send_sem=halo_sends.at[end],
            recv_sem=halo_recvs.at[end],
            device_id=(lax.rem(me + step, peers), side),
            device_id_type=MESH,
        )

    halos = [halo(0, low_ref, 1), halo(1, high_ref, peers - 1)]
    for copy in halos:
        copy.start()
    own = pltpu.make_async_copy(send_ref.at[me], got_ref.at[me * sides + side], own_sem)
    own.start()
    order = [(0, p) for p in range(count)]
    while near or far:
        order += near[:2] + far[:1]
        near, far = near[2:], far[1:]
    for step in range(len(order) + 2):
        if step < len(order):
            item = order[step]
            if item[0] > 0:
                to_owner(*item).wait_recv()
            to_across(*item).start()
            to_beside(*item).start()
            if item in follow:
                to_owner(*item).wait_send()
                to_owner(*follow[item]).start()
        if step >= 2:
            to_across(*order[step - 2]).wait_recv()
            on_beside(*order[step - 2]).start()
    own.wait()
    for copy in halos:
        copy.wait()
    for item in order:
        if item[0] > 0 and item not in follow:
            to_owner(*item).wait_send()
        to_across(*item).wait_send()
        to_beside(*item).wait()
        on_beside(*item).wait()


def route(send, field, peers, sides, room):
    rows, width = send.shape[1:]
    if peers > 16 or room < 2:
        pieces = ((0, rows),)
    else:
        pieces = ((0, room // 2 * width), (room // 2 * width, rows))
    return pl.pallas_call(
        functools.partial(route_kernel, peers, sides, pieces),
        out_shape=[
            jax.ShapeDtypeStruct((SPARE * peers * sides, rows, width), send.dtype),
            jax.ShapeDtypeStruct(field.shape, field.dtype),
            jax.ShapeDtypeStruct(field.shape, field.dtype),
        ],
        in_specs=[pl.BlockSpec(memory_space=pl.ANY)] * 2,
        out_specs=[pl.BlockSpec(memory_space=pltpu.HBM)] + [pl.BlockSpec(memory_space=pl.ANY)] * 2,
        scratch_shapes=[
            pltpu.SemaphoreType.DMA,
            pltpu.SemaphoreType.DMA((4, peers, len(pieces))),
            pltpu.SemaphoreType.DMA((4, peers, len(pieces))),
            pltpu.SemaphoreType.DMA((2,)),
            pltpu.SemaphoreType.DMA((2,)),
        ],
        compiler_params=pltpu.CompilerParams(collective_id=0, has_side_effects=True),
        name="route",
    )(send, field)


def block_list(notes, room, rows_each, local_rows):
    index_bits, col_bits = bits_of(local_rows)
    filled, col, index = [notes[:, i, :room].reshape(-1) for i in range(3)]
    count = filled.shape[0]
    length = -(-(count + local_rows) // GROUP) * GROUP
    key = jnp.where(filled == 1, col, -1)
    items = jnp.arange(count)
    starts = (items // room * rows_each + items % room * notes.shape[2]) // 16
    keys = jnp.arange(local_rows)
    rank = jnp.sum(
        ((key[:, None] == key[None, :]) & (items[None, :] < items[:, None])).astype(jnp.int32), axis=1
    )
    is_key = key[:, None] == keys[None, :]
    even = (jnp.sum(is_key.astype(jnp.int32), axis=0) + 1) // 2 * 2
    first = jnp.sum(jnp.where(keys[:, None] > keys[None, :], even[None, :], 0), axis=1)
    pos = rank + jnp.sum(jnp.where(is_key, first[None, :], 0), axis=1)
    value = ((starts << col_bits) | col) << index_bits | index
    some = jnp.max(jnp.where(filled == 1, starts, 0))
    empty = ((some << col_bits) | local_rows) << index_bits | (3 * local_rows)
    pick = jnp.arange(length)[:, None] == jnp.where(key >= 0, pos, -1)[None, :]
    listed = empty + jnp.sum(jnp.where(pick, value[None, :] - empty, 0), axis=1)
    return jnp.concatenate([listed, jnp.sum(even).reshape(1)])


def add_blocks(first_sweep, list_ref, blocks_ref, packed_ref, ext, acc, buf, sems, local_rows):
    index_bits, col_bits = bits_of(local_rows)
    width = buf.shape[-1]
    chunks = lax.div(list_ref[list_ref.shape[0] - 1] + (GROUP - 1), jnp.int32(GROUP))

    def whole(chunk):
        slot = lax.rem(chunk, BUFFERS)
        return pltpu.make_async_copy(
            packed_ref.at[pl.ds(chunk * GROUP * width, GROUP * width)], buf.at[slot], sems.at[slot, 0]
        )

    def copies(chunk):
        if not first_sweep:
            return [whole(chunk)]
        slot = lax.rem(chunk, BUFFERS)
        out = []
        for g in range(GROUP):
            begin = (list_ref[chunk * GROUP + g] >> (index_bits + col_bits)) * 16
            out.append(
                pltpu.make_async_copy(
                    blocks_ref.at[pl.ds(pl.multiple_of(begin, 16), width)],
                    buf.at[slot, g * width : (g + 1) * width],
                    sems.at[slot, 0],
                )
            )
        return out

    def write(chunk):
        slot = lax.rem(chunk, BUFFERS)
        return pltpu.make_async_copy(
            buf.at[slot], packed_ref.at[pl.ds(chunk * GROUP * width, GROUP * width)], sems.at[slot, 1]
        )

    def start(chunk):
        @pl.when(chunk < chunks)
        def _():
            for copy in copies(chunk):
                copy.start()

    for ahead in range(BUFFERS - 1):
        start(jnp.int32(ahead))

    def body(chunk, carry):
        if first_sweep:

            @pl.when(chunk > 0)
            def _():
                write(chunk - 1).wait()

        start(chunk + (BUFFERS - 1))
        whole(chunk).wait()
        if first_sweep:
            write(chunk).start()
        slot = lax.rem(chunk, BUFFERS)
        mask = (1 << index_bits) - 1
        for begin in range(0, GROUP, 2 * BATCH):
            products = []
            for g in range(begin, begin + 2 * BATCH, 2):
                item = list_ref[chunk * GROUP + g]
                other = list_ref[chunk * GROUP + g + 1]
                rows = jnp.concatenate([ext[item & mask], ext[other & mask]], axis=1)
                pair = buf[slot, g * width : (g + 2) * width]
                col = (item >> index_bits) & ((1 << col_bits) - 1)
                products.append((col, jnp.dot(rows, pair, preferred_element_type=jnp.float32)))
            for col, product in products:
                acc[col] += product
        return carry

    lax.fori_loop(0, chunks, body, 0)
    if first_sweep:

        @pl.when(chunks > 0)
        def _():
            write(chunks - 1).wait()


def sweep_kernel(sweep, list_ref, coef_ref, blocks_ref, low_ref, own_ref, high_ref, res_ref, dir_ref, *rest):
    first_sweep, last = sweep == 0, sweep + 1 == ITERS
    *refs, ext, acc, buf, sems = rest
    packed_ref = refs.pop() if first_sweep else blocks_ref
    if last:
        (res_out,) = refs
    else:
        adj_ref, res_out, dir_out, adj_out, round_out = refs
    rows = res_ref.shape[0]
    acc[0:rows] = res_ref[...] - dir_ref[...]
    ext[0:rows] = low_ref[...]
    ext[rows : 2 * rows] = own_ref[...]
    ext[2 * rows : 3 * rows] = high_ref[...]
    ext[3 * rows] = jnp.zeros_like(ext[0])
    add_blocks(first_sweep, list_ref, blocks_ref, packed_ref, ext, acc, buf, sems, rows)
    res = acc[0:rows]
    res_out[...] = res
    if not last:
        direction = coef_ref[2 * sweep] * dir_ref[...] + coef_ref[2 * sweep + 1] * res
        dir_out[...] = direction
        adj_out[...] = adj_ref[...] + direction
        round_out[...] = direction.astype(jnp.bfloat16)


def halo_kernel(peers, field_ref, low_ref, high_ref, send_sems, recv_sems):
    me, side = lax.axis_index("rows"), lax.axis_index("rhs")
    after, before = lax.rem(me + 1, peers), lax.rem(me + peers - 1, peers)
    barrier = pltpu.get_barrier_semaphore()
    for other in (after, before):
        pl.semaphore_signal(barrier, inc=1, device_id=(other, side), device_id_type=MESH)
    pl.semaphore_wait(barrier, 2)

    def copy(end, ref, other):
        return pltpu.make_async_remote_copy(
            src_ref=field_ref,
            dst_ref=ref,
            send_sem=send_sems.at[end],
            recv_sem=recv_sems.at[end],
            device_id=(other, side),
            device_id_type=MESH,
        )

    copies = [copy(0, low_ref, after), copy(1, high_ref, before)]
    for each in copies:
        each.start()
    for each in copies:
        each.wait()


def halo(field, peers):
    vmem = pl.BlockSpec(memory_space=pltpu.VMEM)
    return pl.pallas_call(
        functools.partial(halo_kernel, peers),
        out_shape=[jax.ShapeDtypeStruct(field.shape, field.dtype)] * 2,
        in_specs=[vmem],
        out_specs=[vmem] * 2,
        scratch_shapes=[pltpu.SemaphoreType.DMA((2,)), pltpu.SemaphoreType.DMA((2,))],
        compiler_params=pltpu.CompilerParams(collective_id=1, has_side_effects=True),
        name="halo",
    )(field)


def local(
    factor_left,
    factor_right,
    state_diag,
    owner,
    col_local,
    row_shift,
    row_local,
    rhs_in,
    low_bound,
    high_bound,
):
    peers = lax.axis_size("rows")
    sides = lax.axis_size("rhs")
    slots = owner.shape[0]
    width = factor_left.shape[1]
    local_rows, columns, _ = rhs_in.shape
    room = min(slots, max(2, 3 * slots // peers))

    places = jnp.concatenate([owner[:, 0], col_local, row_shift * local_rows + row_local])
    send = form(factor_left, factor_right, state_diag, places, peers, room)
    rounded = (rhs_in / ((high_bound[0] + low_bound[0]) / 2.0)).astype(jnp.bfloat16)
    got, low_rows, high_rows = route(send, rounded, peers, sides, room)
    notes = got[: peers * sides, room * width :, :].astype(jnp.int32)
    where = block_list(notes, room, got.shape[1], local_rows)
    packed_rows = (where.shape[0] - 1) * width
    packed_shape = jax.ShapeDtypeStruct((SPARE * packed_rows, width), jnp.bfloat16)

    low = low_bound[0]
    high = high_bound[0]
    theta = (high + low) / 2.0
    delta = (high - low) / 2.0
    sigma = theta / delta
    rho = 1.0 / sigma
    residual = rhs_in
    direction = residual / theta
    adjoint = direction
    coefs = []
    for _ in range(ITERS - 1):
        rho_next = 1.0 / (2.0 * sigma - rho)
        coefs += [rho_next * rho, 2.0 * rho_next / delta]
        rho = rho_next
    coefs = jnp.stack(coefs)

    smem = pl.BlockSpec(memory_space=pltpu.SMEM)
    vmem = pl.BlockSpec(memory_space=pltpu.VMEM)
    hbm = pl.BlockSpec(memory_space=pltpu.HBM)
    field = jax.ShapeDtypeStruct(rhs_in.shape, jnp.float32)
    work = [
        pltpu.VMEM((3 * local_rows + 1, columns, width), jnp.bfloat16),
        pltpu.VMEM((local_rows + 1, columns, width), jnp.float32),
        pltpu.VMEM((BUFFERS, GROUP * width, width), jnp.bfloat16),
        pltpu.SemaphoreType.DMA((BUFFERS, 2)),
    ]
    params = pltpu.CompilerParams(vmem_limit_bytes=VMEM_LIMIT)

    cost = pl.CostEstimate(
        flops=columns * width * packed_rows,
        bytes_accessed=packed_rows * width + 4 * rhs_in.size * 4,
        transcendentals=0,
    )

    blocks = got.reshape(-1, width)
    for sweep in range(ITERS):
        first_sweep, last = sweep == 0, sweep + 1 == ITERS
        if not first_sweep:
            low_rows, high_rows = halo(rounded, peers)
        fields = [residual, direction] if last else [residual, direction, adjoint]
        outs = [field] if last else [field] * 3 + [jax.ShapeDtypeStruct(rhs_in.shape, jnp.bfloat16)]
        result = pl.pallas_call(
            functools.partial(sweep_kernel, sweep),
            out_shape=outs + [packed_shape] * first_sweep,
            in_specs=[smem, smem, hbm] + [vmem] * (3 + len(fields)),
            out_specs=[vmem] * len(outs) + [hbm] * first_sweep,
            scratch_shapes=work,
            compiler_params=params,
            cost_estimate=cost,
            name="sweep",
        )(where, coefs, blocks, low_rows, rounded, high_rows, *fields)
        residual = result[0]
        if first_sweep:
            blocks = result[-1]
        if not last:
            direction, adjoint, rounded = result[1:4]
    return (adjoint, residual)


def solution(mesh):
    placed = (
        P(("rows", "rhs"), None, None),
        P(("rows", "rhs"), None, None),
        P(("rows", "rhs"), None),
        P(("rows", "rhs"), None),
        P(("rows", "rhs")),
        P(("rows", "rhs")),
        P(("rows", "rhs")),
        P("rows", "rhs", None),
        P(),
        P(),
    )
    return jax.shard_map(
        local,
        mesh=mesh,
        in_specs=placed,
        out_specs=(P("rows", "rhs", None), P("rows", "rhs", None)),
        check_vma=False,
    )
```

```python
import functools

import jax
import jax.numpy as jnp
from jax import lax
from jax.experimental import pallas as pl
from jax.experimental.pallas import tpu as pltpu
from jax.sharding import PartitionSpec as P

ITERS = 4
GROUP = 16
BUFFERS = 4
BATCH = 4
VMEM_LIMIT = 40 * 1024 * 1024
VMEM_SMALL = 16 * 1024 * 1024
SPARE = 2
MESH = pl.DeviceIdType.MESH


def bits_of(local_rows):
    return (3 * local_rows).bit_length(), local_rows.bit_length()


def form_kernel(room, left_ref, right_ref, diag_ref, place_ref, send_ref, notes, filled):
    slots, width, _ = left_ref.shape
    peers = send_ref.shape[0]
    notes[...] = jnp.zeros_like(notes)
    for owner in range(peers):
        filled[owner] = 0
    line = lax.broadcasted_iota(jnp.int32, notes.shape[1:], 0)
    lane = lax.broadcasted_iota(jnp.int32, notes.shape[1:], 1)
    for k in range(slots):
        scaled = (diag_ref[:, k : k + 1] * right_ref[k].astype(jnp.float32)).astype(jnp.bfloat16)
        block = jnp.dot(left_ref[k], scaled, preferred_element_type=jnp.float32)
        owner = place_ref[k]
        place = filled[owner]
        filled[owner] = place + 1
        send_ref[owner, pl.ds(pl.multiple_of(place * width, width), width)] = block.astype(jnp.bfloat16)
        col, index = place_ref[slots + k], place_ref[2 * slots + k]
        note = jnp.where(line == 0, 1, jnp.where(line == 1, col, index))
        notes[owner] = jnp.where((lane == place) & (line < 3), note, notes[owner])
    for owner in range(peers):
        send_ref[owner, room * width : room * width + 16] = notes[owner].astype(jnp.float32).astype(jnp.bfloat16)


def form(left, right, diag, places, peers, room):
    slots, width, _ = left.shape
    smem = pl.BlockSpec(memory_space=pltpu.SMEM)
    vmem = pl.BlockSpec(memory_space=pltpu.VMEM)
    return pl.pallas_call(
        functools.partial(form_kernel, room),
        out_shape=jax.ShapeDtypeStruct((peers, room * width + 16, width), jnp.bfloat16),
        in_specs=[vmem, vmem, vmem, smem],
        out_specs=vmem,
        scratch_shapes=[
            pltpu.VMEM((peers, 16, width), jnp.int32),
            pltpu.SMEM((peers,), jnp.int32),
        ],
        compiler_params=pltpu.CompilerParams(vmem_limit_bytes=VMEM_LIMIT),
        name="form",
    )(left, right, diag.T, places)


def route_kernel(
    peers, sides, pieces, send_ref, field_ref, got_ref, near_ref, beyond_ref, own_sem, send_sems, recv_sems, halo_sends, halo_recvs
):
    me, side = lax.axis_index("rows"), lax.axis_index("rhs")
    across, beside = side ^ 2, side ^ 1
    paired = peers & (peers - 1) == 0

    def target(d):
        return me ^ d if paired else lax.rem(me + d, peers)

    def source(d):
        return me ^ d if paired else lax.rem(me - d + peers, peers)

    barrier = pltpu.get_barrier_semaphore()
    for d in range(1, peers):
        pl.semaphore_signal(barrier, inc=1, device_id=(source(d), side), device_id_type=MESH)
    for other in (across, beside):
        pl.semaphore_signal(barrier, inc=1, device_id=(me, other), device_id_type=MESH)
    pl.semaphore_wait(barrier, peers + 1)

    def remote(kind, d, piece, src, slot, device):
        begin, end = pieces[piece]
        return pltpu.make_async_remote_copy(
            src_ref=src.at[begin:end],
            dst_ref=got_ref.at[slot, begin:end],
            send_sem=send_sems.at[kind, d, piece],
            recv_sem=recv_sems.at[kind, d, piece],
            device_id=device,
            device_id_type=MESH,
        )

    def to_owner(d, p):
        return remote(0, d, p, send_ref.at[target(d)], me * sides + side, (target(d), side))

    def held(d):
        return send_ref.at[me] if d == 0 else got_ref.at[source(d) * sides + side]

    def to_across(d, p):
        return remote(1, d, p, held(d), source(d) * sides + side, (me, across))

    def to_beside(d, p):
        return remote(2, d, p, held(d), source(d) * sides + side, (me, beside))

    def on_beside(d, p):
        slot = source(d) * sides + across
        return remote(3, d, p, got_ref.at[slot], slot, (me, beside))

    count = len(pieces)
    near = [(d, p) for d in range(1, peers // 2) for p in range(count)]
    far = [(d, p) for d in range(peers // 2, peers) for p in range(count)]
    follow = {}
    for queue in (near, far):
        follow.update(zip(queue, queue[2:]))
    for item in far[:2] + near[:2]:
        to_owner(*item).start()

    def halo(end, ref, other):
        return pltpu.make_async_remote_copy(
            src_ref=field_ref,
            dst_ref=ref,
            send_sem=halo_sends.at[end],
            recv_sem=halo_recvs.at[end],
            device_id=(other, side),
            device_id_type=MESH,
        )

    odd = lax.rem(me, 2)
    halos = [
        halo(0, near_ref, me + 1 - 2 * odd),
        halo(1, beyond_ref, lax.rem(me - 1 + 2 * odd + peers, peers)),
    ]
    for copy in halos:
        copy.start()
    own = pltpu.make_async_copy(send_ref.at[me], got_ref.at[me * sides + side], own_sem)
    own.start()
    order = [(0, p) for p in range(count)]
    while near or far:
        order += near[:2] + far[:1]
        near, far = near[2:], far[1:]
    for step in range(len(order) + 2):
        if step < len(order):
            item = order[step]
            if item[0] > 0:
                to_owner(*item).wait_recv()
            to_across(*item).start()
            to_beside(*item).start()
            if item in follow:
                to_owner(*item).wait_send()
                to_owner(*follow[item]).start()
        if step >= 2:
            to_across(*order[step - 2]).wait_recv()
            on_beside(*order[step - 2]).start()
    own.wait()
    for copy in halos:
        copy.wait()
    for item in order:
        if item[0] > 0 and item not in follow:
            to_owner(*item).wait_send()
        to_across(*item).wait_send()
        to_beside(*item).wait()
        on_beside(*item).wait()


def route(send, field, peers, sides, room):
    rows, width = send.shape[1:]
    if peers > 16 or room < 2:
        pieces = ((0, rows),)
    else:
        pieces = ((0, room // 2 * width), (room // 2 * width, rows))
    return pl.pallas_call(
        functools.partial(route_kernel, peers, sides, pieces),
        out_shape=[
            jax.ShapeDtypeStruct((SPARE * peers * sides, rows, width), send.dtype),
            jax.ShapeDtypeStruct(field.shape, field.dtype),
            jax.ShapeDtypeStruct(field.shape, field.dtype),
        ],
        in_specs=[pl.BlockSpec(memory_space=pl.ANY)] * 2,
        out_specs=[pl.BlockSpec(memory_space=pltpu.HBM)] + [pl.BlockSpec(memory_space=pl.ANY)] * 2,
        scratch_shapes=[
            pltpu.SemaphoreType.DMA,
            pltpu.SemaphoreType.DMA((4, peers, len(pieces))),
            pltpu.SemaphoreType.DMA((4, peers, len(pieces))),
            pltpu.SemaphoreType.DMA((2,)),
            pltpu.SemaphoreType.DMA((2,)),
        ],
        compiler_params=pltpu.CompilerParams(
            collective_id=0, has_side_effects=True, vmem_limit_bytes=VMEM_LIMIT
        ),
        name="route",
    )(send, field)


def block_list(notes, room, rows_each, local_rows):
    index_bits, col_bits = bits_of(local_rows)
    filled, col, index = [notes[:, i, :room].reshape(-1) for i in range(3)]
    swap = lax.rem(lax.axis_index("rows"), 2) == 0
    index = jnp.where(swap, (2 - index // local_rows) * local_rows + index % local_rows, index)
    count = filled.shape[0]
    length = -(-(count + local_rows) // GROUP) * GROUP
    key = jnp.where(filled == 1, col, -1)
    items = jnp.arange(count)
    starts = (items // room * rows_each + items % room * notes.shape[2]) // 16
    keys = jnp.arange(local_rows)
    rank = jnp.sum(
        ((key[:, None] == key[None, :]) & (items[None, :] < items[:, None])).astype(jnp.int32), axis=1
    )
    is_key = key[:, None] == keys[None, :]
    even = (jnp.sum(is_key.astype(jnp.int32), axis=0) + 1) // 2 * 2
    first = jnp.sum(jnp.where(keys[:, None] > keys[None, :], even[None, :], 0), axis=1)
    pos = rank + jnp.sum(jnp.where(is_key, first[None, :], 0), axis=1)
    value = ((starts << col_bits) | col) << index_bits | index
    some = jnp.max(jnp.where(filled == 1, starts, 0))
    empty = ((some << col_bits) | local_rows) << index_bits | (3 * local_rows)
    pick = jnp.arange(length)[:, None] == jnp.where(key >= 0, pos, -1)[None, :]
    listed = empty + jnp.sum(jnp.where(pick, value[None, :] - empty, 0), axis=1)
    return jnp.concatenate([listed, jnp.sum(even).reshape(1)])


def add_blocks(first_sweep, list_ref, blocks_ref, packed_ref, ext, acc, buf, sems, local_rows):
    index_bits, col_bits = bits_of(local_rows)
    width = buf.shape[-1]
    chunks = lax.div(list_ref[list_ref.shape[0] - 1] + (GROUP - 1), jnp.int32(GROUP))

    def whole(chunk):
        slot = lax.rem(chunk, BUFFERS)
        return pltpu.make_async_copy(
            packed_ref.at[pl.ds(chunk * GROUP * width, GROUP * width)], buf.at[slot], sems.at[slot, 0]
        )

    def copies(chunk):
        if not first_sweep:
            return [whole(chunk)]
        slot = lax.rem(chunk, BUFFERS)
        out = []
        for g in range(GROUP):
            begin = (list_ref[chunk * GROUP + g] >> (index_bits + col_bits)) * 16
            out.append(
                pltpu.make_async_copy(
                    blocks_ref.at[pl.ds(pl.multiple_of(begin, 16), width)],
                    buf.at[slot, g * width : (g + 1) * width],
                    sems.at[slot, 0],
                )
            )
        return out

    def write(chunk):
        slot = lax.rem(chunk, BUFFERS)
        return pltpu.make_async_copy(
            buf.at[slot], packed_ref.at[pl.ds(chunk * GROUP * width, GROUP * width)], sems.at[slot, 1]
        )

    def start(chunk):
        @pl.when(chunk < chunks)
        def _():
            for copy in copies(chunk):
                copy.start()

    for ahead in range(BUFFERS - 1):
        start(jnp.int32(ahead))

    def body(chunk, carry):
        if first_sweep:

            @pl.when(chunk > 0)
            def _():
                write(chunk - 1).wait()

        start(chunk + (BUFFERS - 1))
        whole(chunk).wait()
        if first_sweep:
            write(chunk).start()
        slot = lax.rem(chunk, BUFFERS)
        mask = (1 << index_bits) - 1
        for begin in range(0, GROUP, 2 * BATCH):
            products = []
            for g in range(begin, begin + 2 * BATCH, 2):
                item = list_ref[chunk * GROUP + g]
                other = list_ref[chunk * GROUP + g + 1]
                rows = jnp.concatenate([ext[item & mask], ext[other & mask]], axis=1)
                pair = buf[slot, g * width : (g + 2) * width]
                col = (item >> index_bits) & ((1 << col_bits) - 1)
                products.append((col, jnp.dot(rows, pair, preferred_element_type=jnp.float32)))
            for col, product in products:
                acc[col] += product
        return carry

    lax.fori_loop(0, chunks, body, 0)
    if first_sweep:

        @pl.when(chunks > 0)
        def _():
            write(chunks - 1).wait()


def sweep_kernel(sweep, list_ref, coef_ref, blocks_ref, near_ref, own_ref, beyond_ref, res_ref, dir_ref, *rest):
    first_sweep, last = sweep == 0, sweep + 1 == ITERS
    *refs, ext, acc, buf, sems = rest
    packed_ref = refs.pop() if first_sweep else blocks_ref
    if last:
        (res_out,) = refs
    else:
        adj_ref, res_out, dir_out, adj_out, round_out = refs
    rows = res_ref.shape[0]
    acc[0:rows] = res_ref[...] - dir_ref[...]
    ext[0:rows] = near_ref[...]
    ext[rows : 2 * rows] = own_ref[...]
    ext[2 * rows : 3 * rows] = beyond_ref[...]
    ext[3 * rows] = jnp.zeros_like(ext[0])
    add_blocks(first_sweep, list_ref, blocks_ref, packed_ref, ext, acc, buf, sems, rows)
    res = acc[0:rows]
    res_out[...] = res
    if not last:
        direction = coef_ref[2 * sweep] * dir_ref[...] + coef_ref[2 * sweep + 1] * res
        dir_out[...] = direction
        adj_out[...] = adj_ref[...] + direction
        round_out[...] = direction.astype(jnp.bfloat16)


def halo_kernel(peers, pieces, field_ref, near_ref, beyond_ref, send_sems, recv_sems):
    me, side = lax.axis_index("rows"), lax.axis_index("rhs")
    odd = lax.rem(me, 2)
    partner = me + 1 - 2 * odd
    onward = lax.rem(me + 2 - 4 * odd + peers, peers)
    back = lax.rem(me - 2 + 4 * odd + peers, peers)
    barrier = pltpu.get_barrier_semaphore()
    for other in (partner, back):
        pl.semaphore_signal(barrier, inc=1, device_id=(other, side), device_id_type=MESH)
    pl.semaphore_wait(barrier, 2)
    depth = field_ref.shape[0] // pieces

    def copy(kind, p, src, dst, other):
        return pltpu.make_async_remote_copy(
            src_ref=src.at[p * depth : (p + 1) * depth],
            dst_ref=dst.at[p * depth : (p + 1) * depth],
            send_sem=send_sems.at[kind, p],
            recv_sem=recv_sems.at[kind, p],
            device_id=(other, side),
            device_id_type=MESH,
        )

    first = [copy(0, p, field_ref, near_ref, partner) for p in range(pieces)]
    second = [copy(1, p, near_ref, beyond_ref, onward) for p in range(pieces)]
    for each in first:
        each.start()
    for p in range(pieces):
        first[p].wait_recv()
        second[p].start()
    for p in range(pieces):
        first[p].wait_send()
        second[p].wait()


def halo(field, peers):
    vmem = pl.BlockSpec(memory_space=pltpu.VMEM)
    pieces = 4 if field.shape[0] % 4 == 0 else 1
    return pl.pallas_call(
        functools.partial(halo_kernel, peers, pieces),
        out_shape=[jax.ShapeDtypeStruct(field.shape, field.dtype)] * 2,
        in_specs=[vmem],
        out_specs=[vmem] * 2,
        scratch_shapes=[pltpu.SemaphoreType.DMA((2, pieces)), pltpu.SemaphoreType.DMA((2, pieces))],
        compiler_params=pltpu.CompilerParams(
            collective_id=1, has_side_effects=True, vmem_limit_bytes=VMEM_SMALL
        ),
        name="halo",
    )(field)


def local(
    factor_left,
    factor_right,
    state_diag,
    owner,
    col_local,
    row_shift,
    row_local,
    rhs_in,
    low_bound,
    high_bound,
):
    peers = lax.axis_size("rows")
    sides = lax.axis_size("rhs")
    slots = owner.shape[0]
    width = factor_left.shape[1]
    local_rows, columns, _ = rhs_in.shape
    room = min(slots, max(2, 3 * slots // peers))

    places = jnp.concatenate([owner[:, 0], col_local, row_shift * local_rows + row_local])
    send = form(factor_left, factor_right, state_diag, places, peers, room)
    rounded = (rhs_in / ((high_bound[0] + low_bound[0]) / 2.0)).astype(jnp.bfloat16)
    got, near_rows, beyond_rows = route(send, rounded, peers, sides, room)
    notes = got[: peers * sides, room * width :, :].astype(jnp.int32)
    where = block_list(notes, room, got.shape[1], local_rows)
    packed_rows = (where.shape[0] - 1) * width
    packed_shape = jax.ShapeDtypeStruct((SPARE * packed_rows, width), jnp.bfloat16)

    low = low_bound[0]
    high = high_bound[0]
    theta = (high + low) / 2.0
    delta = (high - low) / 2.0
    sigma = theta / delta
    rho = 1.0 / sigma
    residual = rhs_in
    direction = residual / theta
    adjoint = direction
    coefs = []
    for _ in range(ITERS - 1):
        rho_next = 1.0 / (2.0 * sigma - rho)
        coefs += [rho_next * rho, 2.0 * rho_next / delta]
        rho = rho_next
    coefs = jnp.stack(coefs)

    smem = pl.BlockSpec(memory_space=pltpu.SMEM)
    vmem = pl.BlockSpec(memory_space=pltpu.VMEM)
    hbm = pl.BlockSpec(memory_space=pltpu.HBM)
    field = jax.ShapeDtypeStruct(rhs_in.shape, jnp.float32)
    work = [
        pltpu.VMEM((3 * local_rows + 1, columns, width), jnp.bfloat16),
        pltpu.VMEM((local_rows + 1, columns, width), jnp.float32),
        pltpu.VMEM((BUFFERS, GROUP * width, width), jnp.bfloat16),
        pltpu.SemaphoreType.DMA((BUFFERS, 2)),
    ]
    params = pltpu.CompilerParams(vmem_limit_bytes=VMEM_LIMIT)

    cost = pl.CostEstimate(
        flops=columns * width * packed_rows,
        bytes_accessed=packed_rows * width + 4 * rhs_in.size * 4,
        transcendentals=0,
    )

    blocks = got.reshape(-1, width)
    for sweep in range(ITERS):
        first_sweep, last = sweep == 0, sweep + 1 == ITERS
        if not first_sweep:
            near_rows, beyond_rows = halo(rounded, peers)
        fields = [residual, direction] if last else [residual, direction, adjoint]
        outs = [field] if last else [field] * 3 + [jax.ShapeDtypeStruct(rhs_in.shape, jnp.bfloat16)]
        result = pl.pallas_call(
            functools.partial(sweep_kernel, sweep),
            out_shape=outs + [packed_shape] * first_sweep,
            in_specs=[smem, smem, hbm] + [vmem] * (3 + len(fields)),
            out_specs=[vmem] * len(outs) + [hbm] * first_sweep,
            scratch_shapes=work,
            compiler_params=params,
            cost_estimate=cost,
            name="sweep",
        )(where, coefs, blocks, near_rows, rounded, beyond_rows, *fields)
        residual = result[0]
        if first_sweep:
            blocks = result[-1]
        if not last:
            direction, adjoint, rounded = result[1:4]
    return (adjoint, residual)


def solution(mesh):
    placed = (
        P(("rows", "rhs"), None, None),
        P(("rows", "rhs"), None, None),
        P(("rows", "rhs"), None),
        P(("rows", "rhs"), None),
        P(("rows", "rhs")),
        P(("rows", "rhs")),
        P(("rows", "rhs")),
        P("rows", "rhs", None),
        P(),
        P(),
    )
    return jax.shard_map(
        local,
        mesh=mesh,
        in_specs=placed,
        out_specs=(P("rows", "rhs", None), P("rows", "rhs", None)),
        check_vma=False,
    )
```

```python
import functools

import jax
import jax.numpy as jnp
from jax import lax
from jax.experimental import pallas as pl
from jax.experimental.pallas import tpu as pltpu
from jax.sharding import PartitionSpec as P

ITERS = 4
GROUP = 16
BUFFERS = 4
BATCH = 4
VMEM_LIMIT = 40 * 1024 * 1024
VMEM_SMALL = 16 * 1024 * 1024
SPARE = 2
MESH = pl.DeviceIdType.MESH


def bits_of(local_rows):
    return (3 * local_rows).bit_length(), local_rows.bit_length()


def form_kernel(room, left_ref, right_ref, diag_ref, place_ref, send_ref, notes, filled):
    slots, width, _ = left_ref.shape
    peers = send_ref.shape[0]
    notes[...] = jnp.zeros_like(notes)
    for owner in range(peers):
        filled[owner] = 0
    line = lax.broadcasted_iota(jnp.int32, notes.shape[1:], 0)
    lane = lax.broadcasted_iota(jnp.int32, notes.shape[1:], 1)
    for k in range(slots):
        scaled = (diag_ref[:, k : k + 1] * right_ref[k].astype(jnp.float32)).astype(jnp.bfloat16)
        block = jnp.dot(left_ref[k], scaled, preferred_element_type=jnp.float32)
        owner = place_ref[k]
        place = filled[owner]
        filled[owner] = place + 1
        send_ref[owner, pl.ds(pl.multiple_of(place * width, width), width)] = block.astype(jnp.bfloat16)
        col, index = place_ref[slots + k], place_ref[2 * slots + k]
        note = jnp.where(line == 0, 1, jnp.where(line == 1, col, index))
        notes[owner] = jnp.where((lane == place) & (line < 3), note, notes[owner])
    for owner in range(peers):
        send_ref[owner, room * width : room * width + 16] = notes[owner].astype(jnp.float32).astype(jnp.bfloat16)


def form(left, right, diag, places, peers, room):
    slots, width, _ = left.shape
    smem = pl.BlockSpec(memory_space=pltpu.SMEM)
    vmem = pl.BlockSpec(memory_space=pltpu.VMEM)
    return pl.pallas_call(
        functools.partial(form_kernel, room),
        out_shape=jax.ShapeDtypeStruct((peers, room * width + 16, width), jnp.bfloat16),
        in_specs=[vmem, vmem, vmem, smem],
        out_specs=vmem,
        scratch_shapes=[
            pltpu.VMEM((peers, 16, width), jnp.int32),
            pltpu.SMEM((peers,), jnp.int32),
        ],
        compiler_params=pltpu.CompilerParams(vmem_limit_bytes=VMEM_LIMIT),
        name="form",
    )(left, right, diag.T, places)


def route_kernel(
    peers, sides, pieces, send_ref, field_ref, got_ref, near_ref, beyond_ref, own_sem, send_sems, recv_sems, halo_sends, halo_recvs
):
    me, side = lax.axis_index("rows"), lax.axis_index("rhs")
    across, beside = side ^ 2, side ^ 1
    paired = peers & (peers - 1) == 0

    def target(d):
        return me ^ d if paired else lax.rem(me + d, peers)

    def source(d):
        return me ^ d if paired else lax.rem(me - d + peers, peers)

    barrier = pltpu.get_barrier_semaphore()
    for d in range(1, peers):
        pl.semaphore_signal(barrier, inc=1, device_id=(source(d), side), device_id_type=MESH)
    for other in (across, beside):
        pl.semaphore_signal(barrier, inc=1, device_id=(me, other), device_id_type=MESH)
    pl.semaphore_wait(barrier, peers + 1)

    def remote(kind, d, piece, src, slot, device):
        begin, end = pieces[piece]
        return pltpu.make_async_remote_copy(
            src_ref=src.at[begin:end],
            dst_ref=got_ref.at[slot, begin:end],
            send_sem=send_sems.at[kind, d, piece],
            recv_sem=recv_sems.at[kind, d, piece],
            device_id=device,
            device_id_type=MESH,
        )

    def to_owner(d, p):
        return remote(0, d, p, send_ref.at[target(d)], me * sides + side, (target(d), side))

    def held(d):
        return send_ref.at[me] if d == 0 else got_ref.at[source(d) * sides + side]

    def to_across(d, p):
        return remote(1, d, p, held(d), source(d) * sides + side, (me, across))

    def to_beside(d, p):
        return remote(2, d, p, held(d), source(d) * sides + side, (me, beside))

    def on_beside(d, p):
        slot = source(d) * sides + across
        return remote(3, d, p, got_ref.at[slot], slot, (me, beside))

    count = len(pieces)
    near = [(d, p) for d in range(1, peers // 2) for p in range(count)]
    far = [(d, p) for d in range(peers // 2, peers) for p in range(count)]
    follow = {}
    for queue in (near, far):
        follow.update(zip(queue, queue[2:]))
    for item in far[:2] + near[:2]:
        to_owner(*item).start()

    def halo(end, ref, other):
        return pltpu.make_async_remote_copy(
            src_ref=field_ref,
            dst_ref=ref,
            send_sem=halo_sends.at[end],
            recv_sem=halo_recvs.at[end],
            device_id=(other, side),
            device_id_type=MESH,
        )

    odd = lax.rem(me, 2)
    halos = [
        halo(0, near_ref, me + 1 - 2 * odd),
        halo(1, beyond_ref, lax.rem(me - 1 + 2 * odd + peers, peers)),
    ]
    for copy in halos:
        copy.start()
    own = pltpu.make_async_copy(send_ref.at[me], got_ref.at[me * sides + side], own_sem)
    own.start()
    order = [(0, p) for p in range(count)]
    while near or far:
        order += near[:2] + far[:1]
        near, far = near[2:], far[1:]
    for step in range(len(order) + 2):
        if step < len(order):
            item = order[step]
            if item[0] > 0:
                to_owner(*item).wait_recv()
            to_across(*item).start()
            to_beside(*item).start()
            if item in follow:
                to_owner(*item).wait_send()
                to_owner(*follow[item]).start()
        if step >= 2:
            to_across(*order[step - 2]).wait_recv()
            on_beside(*order[step - 2]).start()
    own.wait()
    for copy in halos:
        copy.wait()
    for item in order:
        if item[0] > 0 and item not in follow:
            to_owner(*item).wait_send()
        to_across(*item).wait_send()
        to_beside(*item).wait()
        on_beside(*item).wait()


def route(send, field, peers, sides, room):
    rows, width = send.shape[1:]
    if peers > 16 or room < 2:
        pieces = ((0, rows),)
    else:
        pieces = ((0, room // 2 * width), (room // 2 * width, rows))
    return pl.pallas_call(
        functools.partial(route_kernel, peers, sides, pieces),
        out_shape=[
            jax.ShapeDtypeStruct((SPARE * peers * sides, rows, width), send.dtype),
            jax.ShapeDtypeStruct(field.shape, field.dtype),
            jax.ShapeDtypeStruct(field.shape, field.dtype),
        ],
        in_specs=[pl.BlockSpec(memory_space=pl.ANY)] * 2,
        out_specs=[pl.BlockSpec(memory_space=pltpu.HBM)] + [pl.BlockSpec(memory_space=pl.ANY)] * 2,
        scratch_shapes=[
            pltpu.SemaphoreType.DMA,
            pltpu.SemaphoreType.DMA((4, peers, len(pieces))),
            pltpu.SemaphoreType.DMA((4, peers, len(pieces))),
            pltpu.SemaphoreType.DMA((2,)),
            pltpu.SemaphoreType.DMA((2,)),
        ],
        compiler_params=pltpu.CompilerParams(
            collective_id=0, has_side_effects=True, vmem_limit_bytes=VMEM_LIMIT
        ),
        name="route",
    )(send, field)


def block_list(notes, room, rows_each, local_rows):
    index_bits, col_bits = bits_of(local_rows)
    filled, col, index = [notes[:, i, :room].reshape(-1) for i in range(3)]
    swap = lax.rem(lax.axis_index("rows"), 2) == 0
    index = jnp.where(swap, (2 - index // local_rows) * local_rows + index % local_rows, index)
    count = filled.shape[0]
    length = -(-(count + local_rows) // GROUP) * GROUP
    key = jnp.where(filled == 1, col, -1)
    items = jnp.arange(count)
    starts = (items // room * rows_each + items % room * notes.shape[2]) // 16
    keys = jnp.arange(local_rows)
    rank = jnp.sum(
        ((key[:, None] == key[None, :]) & (items[None, :] < items[:, None])).astype(jnp.int32), axis=1
    )
    is_key = key[:, None] == keys[None, :]
    even = (jnp.sum(is_key.astype(jnp.int32), axis=0) + 1) // 2 * 2
    first = jnp.sum(jnp.where(keys[:, None] > keys[None, :], even[None, :], 0), axis=1)
    pos = rank + jnp.sum(jnp.where(is_key, first[None, :], 0), axis=1)
    value = ((starts << col_bits) | col) << index_bits | index
    some = jnp.max(jnp.where(filled == 1, starts, 0))
    empty = ((some << col_bits) | local_rows) << index_bits | (3 * local_rows)
    pick = jnp.arange(length)[:, None] == jnp.where(key >= 0, pos, -1)[None, :]
    listed = empty + jnp.sum(jnp.where(pick, value[None, :] - empty, 0), axis=1)
    return jnp.concatenate([listed, jnp.sum(even).reshape(1)])


def add_blocks(first_sweep, list_ref, blocks_ref, packed_ref, ext, acc, buf, sems, local_rows):
    index_bits, col_bits = bits_of(local_rows)
    width = buf.shape[-1]
    chunks = lax.div(list_ref[list_ref.shape[0] - 1] + (GROUP - 1), jnp.int32(GROUP))

    def whole(chunk):
        slot = lax.rem(chunk, BUFFERS)
        return pltpu.make_async_copy(
            packed_ref.at[pl.ds(chunk * GROUP * width, GROUP * width)], buf.at[slot], sems.at[slot, 0]
        )

    def copies(chunk):
        if not first_sweep:
            return [whole(chunk)]
        slot = lax.rem(chunk, BUFFERS)
        out = []
        for g in range(GROUP):
            begin = (list_ref[chunk * GROUP + g] >> (index_bits + col_bits)) * 16
            out.append(
                pltpu.make_async_copy(
                    blocks_ref.at[pl.ds(pl.multiple_of(begin, 16), width)],
                    buf.at[slot, g * width : (g + 1) * width],
                    sems.at[slot, 0],
                )
            )
        return out

    def write(chunk):
        slot = lax.rem(chunk, BUFFERS)
        return pltpu.make_async_copy(
            buf.at[slot], packed_ref.at[pl.ds(chunk * GROUP * width, GROUP * width)], sems.at[slot, 1]
        )

    def start(chunk):
        @pl.when(chunk < chunks)
        def _():
            for copy in copies(chunk):
                copy.start()

    for ahead in range(BUFFERS - 1):
        start(jnp.int32(ahead))

    def body(chunk, carry):
        if first_sweep:

            @pl.when(chunk > 0)
            def _():
                write(chunk - 1).wait()

        start(chunk + (BUFFERS - 1))
        whole(chunk).wait()
        if first_sweep:
            write(chunk).start()
        slot = lax.rem(chunk, BUFFERS)
        mask = (1 << index_bits) - 1
        for begin in range(0, GROUP, 2 * BATCH):
            products = []
            for g in range(begin, begin + 2 * BATCH, 2):
                item = list_ref[chunk * GROUP + g]
                other = list_ref[chunk * GROUP + g + 1]
                rows = jnp.concatenate([ext[item & mask], ext[other & mask]], axis=1)
                pair = buf[slot, g * width : (g + 2) * width]
                col = (item >> index_bits) & ((1 << col_bits) - 1)
                products.append((col, jnp.dot(rows, pair, preferred_element_type=jnp.float32)))
            for col, product in products:
                acc[col] += product
        return carry

    lax.fori_loop(0, chunks, body, 0)
    if first_sweep:

        @pl.when(chunks > 0)
        def _():
            write(chunks - 1).wait()


def sweep_kernel(sweep, list_ref, coef_ref, blocks_ref, near_ref, own_ref, beyond_ref, res_ref, dir_ref, *rest):
    first_sweep, last = sweep == 0, sweep + 1 == ITERS
    *refs, ext, acc, buf, sems = rest
    packed_ref = refs.pop() if first_sweep else blocks_ref
    if last:
        (res_out,) = refs
    else:
        adj_ref, res_out, dir_out, adj_out, round_out = refs
    rows = res_ref.shape[0]
    acc[0:rows] = res_ref[...] - dir_ref[...]
    ext[0:rows] = near_ref[...]
    ext[rows : 2 * rows] = own_ref[...]
    ext[2 * rows : 3 * rows] = beyond_ref[...]
    ext[3 * rows] = jnp.zeros_like(ext[0])
    add_blocks(first_sweep, list_ref, blocks_ref, packed_ref, ext, acc, buf, sems, rows)
    res = acc[0:rows]
    res_out[...] = res
    if not last:
        direction = coef_ref[2 * sweep] * dir_ref[...] + coef_ref[2 * sweep + 1] * res
        dir_out[...] = direction
        adj_out[...] = adj_ref[...] + direction
        round_out[...] = direction.astype(jnp.bfloat16)


def halo_kernel(peers, pieces, field_ref, near_ref, beyond_ref, send_sems, recv_sems):
    me, side = lax.axis_index("rows"), lax.axis_index("rhs")
    odd = lax.rem(me, 2)
    partner = me + 1 - 2 * odd
    onward = lax.rem(me + 2 - 4 * odd + peers, peers)
    back = lax.rem(me - 2 + 4 * odd + peers, peers)
    barrier = pltpu.get_barrier_semaphore()
    for other in (partner, back):
        pl.semaphore_signal(barrier, inc=1, device_id=(other, side), device_id_type=MESH)
    pl.semaphore_wait(barrier, 2)
    depth = field_ref.shape[0] // pieces

    def copy(kind, p, src, dst, other):
        return pltpu.make_async_remote_copy(
            src_ref=src.at[p * depth : (p + 1) * depth],
            dst_ref=dst.at[p * depth : (p + 1) * depth],
            send_sem=send_sems.at[kind, p],
            recv_sem=recv_sems.at[kind, p],
            device_id=(other, side),
            device_id_type=MESH,
        )

    first = [copy(0, p, field_ref, near_ref, partner) for p in range(pieces)]
    second = [copy(1, p, near_ref, beyond_ref, onward) for p in range(pieces)]
    for each in first:
        each.start()
    for p in range(pieces):
        first[p].wait_recv()
        second[p].start()
    for p in range(pieces):
        first[p].wait_send()
        second[p].wait()


def halo(field, peers):
    vmem = pl.BlockSpec(memory_space=pltpu.VMEM)
    pieces = 8 if field.shape[0] % 8 == 0 else 1
    return pl.pallas_call(
        functools.partial(halo_kernel, peers, pieces),
        out_shape=[jax.ShapeDtypeStruct(field.shape, field.dtype)] * 2,
        in_specs=[vmem],
        out_specs=[vmem] * 2,
        scratch_shapes=[pltpu.SemaphoreType.DMA((2, pieces)), pltpu.SemaphoreType.DMA((2, pieces))],
        compiler_params=pltpu.CompilerParams(
            collective_id=1, has_side_effects=True, vmem_limit_bytes=VMEM_SMALL
        ),
        name="halo",
    )(field)


def local(
    factor_left,
    factor_right,
    state_diag,
    owner,
    col_local,
    row_shift,
    row_local,
    rhs_in,
    low_bound,
    high_bound,
):
    peers = lax.axis_size("rows")
    sides = lax.axis_size("rhs")
    slots = owner.shape[0]
    width = factor_left.shape[1]
    local_rows, columns, _ = rhs_in.shape
    room = min(slots, max(2, 3 * slots // peers))

    places = jnp.concatenate([owner[:, 0], col_local, row_shift * local_rows + row_local])
    send = form(factor_left, factor_right, state_diag, places, peers, room)
    rounded = (rhs_in / ((high_bound[0] + low_bound[0]) / 2.0)).astype(jnp.bfloat16)
    got, near_rows, beyond_rows = route(send, rounded, peers, sides, room)
    notes = got[: peers * sides, room * width :, :].astype(jnp.int32)
    where = block_list(notes, room, got.shape[1], local_rows)
    packed_rows = (where.shape[0] - 1) * width
    packed_shape = jax.ShapeDtypeStruct((SPARE * packed_rows, width), jnp.bfloat16)

    low = low_bound[0]
    high = high_bound[0]
    theta = (high + low) / 2.0
    delta = (high - low) / 2.0
    sigma = theta / delta
    rho = 1.0 / sigma
    residual = rhs_in
    direction = residual / theta
    adjoint = direction
    coefs = []
    for _ in range(ITERS - 1):
        rho_next = 1.0 / (2.0 * sigma - rho)
        coefs += [rho_next * rho, 2.0 * rho_next / delta]
        rho = rho_next
    coefs = jnp.stack(coefs)

    smem = pl.BlockSpec(memory_space=pltpu.SMEM)
    vmem = pl.BlockSpec(memory_space=pltpu.VMEM)
    hbm = pl.BlockSpec(memory_space=pltpu.HBM)
    field = jax.ShapeDtypeStruct(rhs_in.shape, jnp.float32)
    work = [
        pltpu.VMEM((3 * local_rows + 1, columns, width), jnp.bfloat16),
        pltpu.VMEM((local_rows + 1, columns, width), jnp.float32),
        pltpu.VMEM((BUFFERS, GROUP * width, width), jnp.bfloat16),
        pltpu.SemaphoreType.DMA((BUFFERS, 2)),
    ]
    params = pltpu.CompilerParams(vmem_limit_bytes=VMEM_LIMIT)

    cost = pl.CostEstimate(
        flops=columns * width * packed_rows,
        bytes_accessed=packed_rows * width + 4 * rhs_in.size * 4,
        transcendentals=0,
    )

    blocks = got.reshape(-1, width)
    for sweep in range(ITERS):
        first_sweep, last = sweep == 0, sweep + 1 == ITERS
        if not first_sweep:
            near_rows, beyond_rows = halo(rounded, peers)
        fields = [residual, direction] if last else [residual, direction, adjoint]
        outs = [field] if last else [field] * 3 + [jax.ShapeDtypeStruct(rhs_in.shape, jnp.bfloat16)]
        result = pl.pallas_call(
            functools.partial(sweep_kernel, sweep),
            out_shape=outs + [packed_shape] * first_sweep,
            in_specs=[smem, smem, hbm] + [vmem] * (3 + len(fields)),
            out_specs=[vmem] * len(outs) + [hbm] * first_sweep,
            scratch_shapes=work,
            compiler_params=params,
            cost_estimate=cost,
            name="sweep",
        )(where, coefs, blocks, near_rows, rounded, beyond_rows, *fields)
        residual = result[0]
        if first_sweep:
            blocks = result[-1]
        if not last:
            direction, adjoint, rounded = result[1:4]
    return (adjoint, residual)


def solution(mesh):
    placed = (
        P(("rows", "rhs"), None, None),
        P(("rows", "rhs"), None, None),
        P(("rows", "rhs"), None),
        P(("rows", "rhs"), None),
        P(("rows", "rhs")),
        P(("rows", "rhs")),
        P(("rows", "rhs")),
        P("rows", "rhs", None),
        P(),
        P(),
    )
    return jax.shard_map(
        local,
        mesh=mesh,
        in_specs=placed,
        out_specs=(P("rows", "rhs", None), P("rows", "rhs", None)),
        check_vma=False,
    )
```
